512 devices in a mesh: node: 64 (over x, y, core), head: 8 (over z).
Axes of the slice: x: 4, y: 8, z: 8, core: 2. Of those that a mesh axis runs over, the one named last changes fastest.
Arguments:
- features: bfloat16 [262144, 512], P(('node', 'head')), may hold values from -8 to 8
- w_query: bfloat16 [512, 512], replicated, may hold values from -0.25 to 0.25
- w_key_value: bfloat16 [512, 2, 512], replicated, may hold values from -0.25 to 0.25
- edge_local: float32 [512], P('head'), may hold values from 0.5 to 2
- edge_expand: float32 [512], P('head'), may hold values from 0.5 to 2
- local_cols: int32 [2048, 8], P('node'), may hold values from 0 to 35, as said below
- exp_rows: int32 [64, 4, 16], P('node'), may hold values from 0 to 31
- exp_cols: int32 [64, 4, 16], P('node'), may hold values from 0 to 31
Outputs:
- attention: bfloat16 [262144, 512], P(('node', 'head'))
The draws below stay inside these ranges and needn't reach their ends.
Inputs may be any that keep to these rules, and one draw needn't show every extreme that they name: `local_cols`: the first slot of every row names a tile of the row's own node block, a value from 2 to 33.
All inputs are finite; a program needn't handle non-finite values.
Results may differ from the reference program's by a relative error of at most 0.009.
Values may be sent and summed in bfloat16 or wider, within the bound.
A program may use at most 64 MiB of HBM per device.

```python
import math
import jax
import jax.numpy as jnp
from jax import lax

D = 512
HEADS = 8
HDIM = 64
TILE = 128
RT = 32
HT = 2
LPR = 8
MATCH = 4
ET = 16
ROWS = 4096
NODES = 262144
N_NODE = 64


def draw_local_cols(key, part):
    key = jax.random.fold_in(key, 11)
    first_key, rest_key = jax.random.split(key)
    first = jax.random.randint(first_key, (NODES // TILE, 1), HT, HT + RT)
    rest = jax.random.randint(rest_key, (NODES // TILE, LPR - 1), 0, RT + 2 * HT)
    return jnp.concatenate([first, rest], axis=1).astype(jnp.int32)


def with_ends(entries, own_key, smallest, high):
    shape = entries.shape
    spot = [jax.random.randint(jax.random.fold_in(own_key, axis), (), 0, shape[axis]) for axis in range(len(shape))]
    entries = entries.at[tuple(spot)].set(smallest)
    longest = shape.index(max(shape))
    spot[longest] = (spot[longest] + 1) % shape[longest]
    return entries.at[tuple(spot)].set(high)


def shard_levels(stream_key, extent, cuts, smallest, top_value):
    factor_of, own = 1.0, jax.random.fold_in(stream_key, 6)
    for position, parts in cuts:
        heights = jnp.exp(jax.random.uniform(jax.random.fold_in(own, position), (parts,), jnp.float32, smallest / len(cuts), top_value / len(cuts)))
        factor_of = factor_of * jnp.repeat(heights, extent[position] // parts).reshape([-1 if axis == position else 1 for axis in range(len(extent))])
    return factor_of


def gaussian(own_key, shape, width, most, cuts=(), kind=jnp.bfloat16):
    values = jax.random.normal(own_key, shape, jnp.float32) * width
    if len(cuts) > 0:
        values = shard_levels(own_key, shape, cuts, -0.22, 0.18) * values
    return jnp.clip(values, min=-most, max=most).astype(kind)


def setup_inputs(seed: int = 0) -> dict:
    key_list = jax.random.split(jax.random.key(seed), 9)
    return {
        "features": gaussian(key_list[0], (NODES, D), 1.0, 8.0, ((0, 512),)),
        "w_query": gaussian(key_list[1], (D, D), D ** -0.5, 0.25),
        "w_key_value": gaussian(key_list[2], (D, 2, D), D ** -0.5, 0.25),
        "edge_local": jnp.clip(jnp.exp(math.log(2.0) - 1.3862944 * jax.random.uniform(key_list[3], (D,), jnp.float32) ** shard_levels(key_list[3], (D,), ((0, 8),), -0.2, 0.2)), 0.5, 2.0),
        "edge_expand": jnp.clip(jnp.exp(math.log(2.0) - 1.3862944 * jax.random.uniform(key_list[4], (D,), jnp.float32) ** shard_levels(key_list[4], (D,), ((0, 8),), -0.2, 0.2)), 0.5, 2.0),
        "local_cols": draw_local_cols(jax.random.fold_in(key_list[8], 71), 0),
        "exp_rows": with_ends(jax.random.randint(key_list[6], (N_NODE, MATCH, ET), 0, RT), jax.random.fold_in(key_list[6], 1), 0, RT - 1).astype(jnp.int32),
        "exp_cols": with_ends(jax.random.randint(key_list[7], (N_NODE, MATCH, ET), 0, RT), jax.random.fold_in(key_list[7], 1), 0, RT - 1).astype(jnp.int32),
    }


highest = lax.Precision.HIGHEST

def attend(queries, key_block, value_block, usable):
    scores = jnp.einsum('gqhe,gkhe->ghqk', queries.astype(jnp.float32), key_block.astype(jnp.float32), precision=highest)
    weights = jnp.exp(jnp.clip(scores, -5.0, 5.0))
    weights = jnp.where(usable[:, None, None, :], weights, jnp.zeros_like(weights))
    denominator = lax.optimization_barrier(jnp.sum(weights, axis=3))
    rounded = lax.optimization_barrier(weights.astype(jnp.bfloat16)).astype(jnp.float32)
    numerator = jnp.einsum('ghqk,gkhe->gqhe', rounded, value_block.astype(jnp.float32), precision=highest)
    return (numerator, jnp.transpose(denominator, (0, 2, 1)))

def local_part(queries, extended, columns, first_tile, tile_count, tile_rows, halo_tiles):
    row_count, head_count, head_width = queries.shape
    row_tiles = row_count // tile_rows
    group_size = min(row_tiles, max(1, 512 // tile_rows))
    group_count = row_tiles // group_size
    ext_tiles = extended.reshape(-1, tile_rows, extended.shape[1])
    grouped_queries = queries.reshape(group_count, group_size, tile_rows, head_count, head_width)
    grouped_columns = columns.reshape(group_count, group_size, columns.shape[1])

    def one_group(pair):
        block_queries, block_columns = pair
        picked = ext_tiles[block_columns].reshape(group_size, -1, 2, head_count, head_width)
        global_tile = first_tile + block_columns - halo_tiles
        usable = jnp.logical_and(global_tile >= 0, global_tile < tile_count)
        usable = jnp.repeat(usable, tile_rows, axis=1)
        return attend(block_queries, picked[:, :, 0], picked[:, :, 1], usable)
    numerator, denominator = lax.map(one_group, (grouped_queries, grouped_columns))
    return (numerator.reshape(row_count, head_count, head_width), denominator.reshape(row_count, head_count))

def expander_part(queries, key_tiles, row_index):
    row_count, head_count, head_width = queries.shape
    tile_rows = key_tiles.shape[1]
    row_tiles = row_count // tile_rows
    pair_count = key_tiles.shape[0]
    chosen = queries.reshape(row_tiles, tile_rows, head_count, head_width)[row_index]
    pairs = key_tiles.reshape(pair_count, tile_rows, 2, head_count, head_width)
    usable = jnp.ones((pair_count, tile_rows), dtype=jnp.bool_)
    numerator, denominator = attend(chosen, pairs[:, :, 0], pairs[:, :, 1], usable)
    selector = (row_index[None, :] == jnp.arange(row_tiles, dtype=jnp.int32)[:, None]).astype(jnp.float32)
    numerator = jnp.einsum('te,eqhw->tqhw', selector, numerator, precision=highest)
    denominator = jnp.einsum('te,eqh->tqh', selector, denominator, precision=highest)
    return (numerator.reshape(row_count, head_count, head_width), denominator.reshape(row_count, head_count))

def reference(features, w_query, w_key_value, edge_local, edge_expand, local_cols, exp_rows, exp_cols):
    scale = 1.0 / math.sqrt(HDIM)
    queries = jnp.dot(features, w_query, preferred_element_type=jnp.float32).astype(jnp.bfloat16)
    key_values = jnp.dot(features, w_key_value.reshape(D, 2 * D), preferred_element_type=jnp.float32).astype(jnp.bfloat16)
    query_wide = lax.optimization_barrier(queries).astype(jnp.float32)
    local_q = (query_wide * edge_local * scale).astype(jnp.bfloat16).reshape(NODES, HEADS, HDIM)
    expand_q = (query_wide * edge_expand * scale).astype(jnp.bfloat16).reshape(NODES, HEADS, HDIM)
    margin = HT * TILE
    padded = jnp.pad(key_values, ((margin, margin), (0, 0)))
    log_count = N_NODE.bit_length() - 1
    tile_count = N_NODE * RT

    def one_block(block):
        start = block * ROWS
        block_local = lax.dynamic_slice_in_dim(local_q, start, ROWS, 0)
        block_expand = lax.dynamic_slice_in_dim(expand_q, start, ROWS, 0)
        extended = lax.dynamic_slice_in_dim(padded, start, ROWS + 2 * margin, 0)
        columns = lax.dynamic_slice_in_dim(local_cols, block * RT, RT, 0)
        numerator, denominator = local_part(block_local, extended, columns, block * RT, tile_count, TILE, HT)
        tile_list = []
        row_list = []
        for matching in range(MATCH):
            partner = jnp.bitwise_xor(block, jnp.int32(1 << matching * log_count // 4))
            partner_block = lax.dynamic_slice_in_dim(key_values, partner * ROWS, ROWS, 0).reshape(RT, TILE, 2 * D)
            tile_list.append(partner_block[exp_cols[block, matching]])
            row_list.append(exp_rows[block, matching])
        extra_num, extra_den = expander_part(block_expand, jnp.concatenate(tile_list, axis=0), jnp.concatenate(row_list, axis=0))
        result = (numerator + extra_num) / (denominator + extra_den)[:, :, None]
        return result.astype(jnp.bfloat16).reshape(ROWS, D)
    blocks = lax.map(one_block, jnp.arange(N_NODE, dtype=jnp.int32))
    return blocks.reshape(NODES, D)
```

```python
import functools
import math

import jax
import jax.numpy as jnp
from jax import lax
from jax.experimental import pallas as pl
from jax.experimental.pallas import tpu as pltpu
from jax.sharding import PartitionSpec as P

HEADS = 8
HDIM = 64
D = 512
TILE = 128
HT = 2
LPR = 8
MATCH = 4
ET = 16
RT = 32
CHUNK = 4
NODES = 64
MESH = pl.DeviceIdType.MESH
F32 = jnp.float32
BF16 = jnp.bfloat16
DISTANCES = (4, 3, 5, 2, 6, 1, 7)
BITS = tuple(m * 6 // 4 for m in range(MATCH))
ROWS_AT = RT * LPR
LAST_AT = ROWS_AT + MATCH * ET
HAS_AT = LAST_AT + MATCH * RT
SAME_AT = HAS_AT + MATCH * RT


def low_lanes(rows):
    return lax.broadcasted_iota(jnp.int32, (rows, TILE), 1) < HDIM


def half_turn(x):
    return pltpu.roll(x, HDIM, 1)


def contract_last(a, b):
    return lax.dot_general(a, b, (((1,), (1,)), ((), ())), preferred_element_type=F32)


def weigh(q, keys):
    return jnp.exp(jnp.clip(contract_last(q, keys), -5.0, 5.0)).astype(BF16)


def with_ones(kv):
    return jnp.where(low_lanes(kv.shape[0]), jnp.ones_like(kv), kv)


def kernel(
    table, feat, w_q, w_kv, edges, cols_out, out,
    send_kv, send_q, kv, halo, vo, q_in, q_local, q_expand, cols_in, cols_smem,
    send_x, kv_x, acc, seg, send_o, o_in,
    kv_ss, kv_rs, q_ss, q_rs, c_ss, c_rs, c_local, h_ss, h_rs, x_ss, x_rs, o_ss, o_rs,
):
    node = lax.axis_index("node")
    me = lax.axis_index("head")

    def around(d):
        return lax.rem(me + d, HEADS)

    def on_z(d):
        return (node, around(d))

    def matched(m):
        return (lax.bitwise_xor(node, jnp.int32(1 << BITS[m])), me)

    def beside(d):
        return (lax.rem(node + d + NODES, NODES), me)

    barrier = pltpu.get_barrier_semaphore()
    greeted = [on_z(d) for d in DISTANCES]
    greeted += [matched(m) for m in range(MATCH)]
    greeted += [beside(1), beside(-1)]
    for device in greeted:
        pl.semaphore_signal(barrier, inc=1, device_id=device, device_id_type=MESH)

    features = feat[...]
    low = low_lanes(CHUNK * TILE)
    for pair in range(HEADS // 2):
        keys = jnp.dot(features, w_kv[:, pair * TILE : (pair + 1) * TILE], preferred_element_type=F32)
        values = jnp.dot(features, w_kv[:, D + pair * TILE : D + (pair + 1) * TILE], preferred_element_type=F32)
        first = jnp.where(low, keys, half_turn(values)).astype(BF16)
        second = jnp.where(low, half_turn(keys), values).astype(BF16)
        send_kv[2 * pair] = first.reshape(CHUNK, TILE, TILE)
        send_kv[2 * pair + 1] = second.reshape(CHUNK, TILE, TILE)

    pl.semaphore_wait(barrier, len(greeted))

    col_copies = []
    for m in range(MATCH):
        copy = pltpu.make_async_remote_copy(
            src_ref=cols_out.at[m], dst_ref=cols_in.at[m], send_sem=c_ss.at[m], recv_sem=c_rs.at[m],
            device_id=matched(m), device_id_type=MESH)
        copy.start()
        col_copies.append(copy)

    def z_copies(src, dst_of, send_sems, recv_sems):
        copies = []
        for i, d in enumerate(DISTANCES):
            copies.append(pltpu.make_async_remote_copy(
                src_ref=src.at[around(d)], dst_ref=dst_of(me), send_sem=send_sems.at[i], recv_sem=recv_sems.at[i],
                device_id=on_z(d), device_id_type=MESH))
        return copies

    kv_copies = z_copies(send_kv, lambda z: kv.at[pl.ds(HT + CHUNK * z, CHUNK)], kv_ss, kv_rs)
    for copy in kv_copies:
        copy.start()
    kv[pl.ds(HT + CHUNK * me, CHUNK)] = send_kv[me]

    half = CHUNK * TILE // 2
    low_half = low_lanes(half)
    for pair in range(HEADS // 2):
        queries = jnp.dot(features, w_q[:, pair * TILE : (pair + 1) * TILE], preferred_element_type=F32)
        top, bottom = queries[:half], queries[half:]
        send_q[2 * pair] = jnp.where(low_half, top, half_turn(bottom)).astype(BF16)
        send_q[2 * pair + 1] = jnp.where(low_half, half_turn(top), bottom).astype(BF16)
    q_copies = z_copies(send_q, lambda z: q_in.at[z], q_ss, q_rs)
    q_in[me] = send_q[me]

    for m in range(MATCH):
        col_copies[m].wait()
        local = pltpu.make_async_copy(cols_in.at[m], cols_smem.at[m], c_local.at[m])
        local.start()
        local.wait()

    for copy in kv_copies:
        copy.wait()

    halo_copies = [
        pltpu.make_async_remote_copy(
            src_ref=kv.at[pl.ds(RT, HT)], dst_ref=halo.at[0], send_sem=h_ss.at[0], recv_sem=h_rs.at[0],
            device_id=beside(1), device_id_type=MESH),
        pltpu.make_async_remote_copy(
            src_ref=kv.at[pl.ds(HT, HT)], dst_ref=halo.at[1], send_sem=h_ss.at[1], recv_sem=h_rs.at[1],
            device_id=beside(-1), device_id_type=MESH),
    ]
    x_copies = {}
    for m in (2, 1, 3, 0):
        def gather(i, carry, m=m):
            send_x[m, i] = kv[HT + cols_smem[m, 0, i]]
            return carry

        lax.fori_loop(0, ET, gather, 0)
        copy = pltpu.make_async_remote_copy(
            src_ref=send_x.at[m], dst_ref=kv_x.at[m], send_sem=x_ss.at[m], recv_sem=x_rs.at[m],
            device_id=matched(m), device_id_type=MESH)
        copy.start()
        x_copies[m] = copy
    for copy in halo_copies:
        copy.start()
    for copy in q_copies:
        copy.start()

    def own_values(i, carry):
        vo[HT + i] = with_ones(kv[HT + i])
        return carry

    lax.fori_loop(0, RT, own_values, 0)

    for copy in halo_copies:
        copy.wait()
    kv[:HT] = halo[0]
    kv[HT + RT :] = halo[1]
    inside = (jnp.where(node > 0, 1.0, 0.0).astype(F32), jnp.where(node < NODES - 1, 1.0, 0.0).astype(F32))
    for i in range(HT):
        vo[i] = (with_ones(kv[i]).astype(F32) * inside[0]).astype(BF16)
        vo[HT + RT + i] = (with_ones(kv[HT + RT + i]).astype(F32) * inside[1]).astype(BF16)

    for copy in q_copies:
        copy.wait()

    def unpack(z, carry):
        packed = q_in[z].astype(F32)
        turned = half_turn(packed)
        for row, target in ((0, q_local), (1, q_expand)):
            scaling = jnp.broadcast_to(edges[row : row + 1, :], (half, TILE))
            for part, source in ((0, packed), (1, turned)):
                scaled = jnp.where(low_half, source * scaling, 0.0).astype(BF16)
                target[pl.ds(CHUNK * z + 2 * part, 2)] = scaled.reshape(2, TILE, TILE)
        return carry

    lax.fori_loop(0, HEADS, unpack, 0)

    def local_tile(t, carry):
        q = q_local[t]
        total = jnp.zeros((TILE, TILE), F32)
        for s in range(0, LPR, 2):
            first, second = table[t * LPR + s], table[t * LPR + s + 1]
            keys = jnp.concatenate([kv[first], kv[second]], axis=0)
            values = jnp.concatenate([vo[first], vo[second]], axis=0)
            total += jnp.dot(weigh(q, keys), values, preferred_element_type=F32)
        acc[t] = total
        return carry

    lax.fori_loop(0, RT, local_tile, 0)

    for m in (0, 3, 1, 2):
        x_copies[m].wait()

        def expander_tile(i, running, m=m):
            q = q_expand[table[ROWS_AT + m * ET + i]]
            keys = kv_x[m, i]
            same = table[SAME_AT + m * ET + i].astype(F32)
            running = running * same + jnp.dot(weigh(q, keys), with_ones(keys), preferred_element_type=F32)
            seg[m, i] = running
            return running

        lax.fori_loop(0, ET, expander_tile, jnp.zeros((TILE, TILE), F32))

    def finish(z, carry):
        tiles = []
        for i in range(CHUNK):
            t = CHUNK * z + i
            total = acc[t]
            for m in range(MATCH):
                has = table[HAS_AT + m * RT + t].astype(F32)
                total += seg[m, table[LAST_AT + m * RT + t]] * has
            tiles.append(total / half_turn(total))
        top = half_turn(jnp.concatenate(tiles[:2], axis=0))
        bottom = jnp.concatenate(tiles[2:], axis=0)
        send_o[z] = jnp.where(low_half, top, bottom).astype(BF16)
        return carry

    o_copies = z_copies(send_o, lambda z: o_in.at[z], o_ss, o_rs)
    for i, d in enumerate(DISTANCES):
        finish(around(d), 0)
        o_copies[i].start()
    finish(me, 0)
    o_in[me] = send_o[me]
    for copy in o_copies:
        copy.wait()
    for pair in range(HEADS // 2):
        a, b = o_in[2 * pair].astype(F32), o_in[2 * pair + 1].astype(F32)
        out[:half, pair * TILE : (pair + 1) * TILE] = jnp.where(low_half, a, half_turn(b)).astype(BF16)
        out[half:, pair * TILE : (pair + 1) * TILE] = jnp.where(low_half, half_turn(a), b).astype(BF16)


def tables(local_cols, exp_rows, exp_cols):
    rows, cols = exp_rows[0], exp_cols[0]
    spot = jnp.arange(ET, dtype=jnp.int32)
    before = (rows[:, None, :] < rows[:, :, None]) | (
        (rows[:, None, :] == rows[:, :, None]) & (spot[None, None, :] < spot[None, :, None]))
    rank = jnp.sum(before.astype(jnp.int32), axis=2)
    place = (rank[:, None, :] == spot[None, :, None]).astype(jnp.int32)
    rows = jnp.sum(place * rows[:, None, :], axis=2)
    cols = jnp.sum(place * cols[:, None, :], axis=2)
    same = jnp.concatenate([jnp.zeros((MATCH, 1), jnp.int32), (rows[:, 1:] == rows[:, :-1]).astype(jnp.int32)], axis=1)
    tiles = jnp.arange(RT, dtype=jnp.int32)
    hits = rows[:, None, :] == tiles[None, :, None]
    has = jnp.max(hits.astype(jnp.int32), axis=2)
    last = jnp.max(jnp.where(hits, spot[None, None, :], 0), axis=2)
    table = jnp.concatenate([part.reshape(-1) for part in (local_cols, rows, last, has, same)])
    cols_out = jnp.zeros((MATCH, 8, TILE), jnp.int32).at[:, 0, :ET].set(cols)
    return table, cols_out


def local(features, w_query, w_key_value, edge_local, edge_expand, local_cols, exp_rows, exp_cols):
    scale = 1.0 / math.sqrt(HDIM)
    edges = jnp.stack([edge_local, edge_expand]) * scale
    edges = jnp.concatenate([edges, edges], axis=1)
    table, cols_out = tables(local_cols, exp_rows, exp_cols)
    vmem = pl.BlockSpec(memory_space=pltpu.VMEM)
    n = len(DISTANCES)
    half = CHUNK * TILE // 2
    dma = pltpu.SemaphoreType.DMA
    return pl.pallas_call(
        kernel,
        name="exphormer",
        out_shape=jax.ShapeDtypeStruct((CHUNK * TILE, D), BF16),
        in_specs=[pl.BlockSpec(memory_space=pltpu.SMEM)] + [vmem] * 5,
        out_specs=vmem,
        scratch_shapes=[
            pltpu.VMEM((HEADS, CHUNK, TILE, TILE), BF16),
            pltpu.VMEM((HEADS, half, TILE), BF16),
            pltpu.VMEM((RT + 2 * HT, TILE, TILE), BF16),
            pltpu.VMEM((2, HT, TILE, TILE), BF16),
        pltpu.VMEM((RT + 2 * HT, TILE, TILE), BF16),
            pltpu.VMEM((HEADS, half, TILE), BF16),
            pltpu.VMEM((RT, TILE, TILE), BF16),
            pltpu.VMEM((RT, TILE, TILE), BF16),
            pltpu.VMEM((MATCH, 8, TILE), jnp.int32),
            pltpu.SMEM((MATCH, 8, TILE), jnp.int32),
            pltpu.VMEM((MATCH, ET, TILE, TILE), BF16),
            pltpu.VMEM((MATCH, ET, TILE, TILE), BF16),
            pltpu.VMEM((RT, TILE, TILE), F32),
            pltpu.VMEM((MATCH, ET, TILE, TILE), F32),
            pltpu.VMEM((HEADS, half, TILE), BF16),
            pltpu.VMEM((HEADS, half, TILE), BF16),
            dma((n,)), dma((n,)), dma((n,)), dma((n,)),
            dma((MATCH,)), dma((MATCH,)), dma((MATCH,)),
            dma((2,)), dma((2,)), dma((MATCH,)), dma((MATCH,)), dma((n,)), dma((n,)),
        ],
        compiler_params=pltpu.CompilerParams(
            collective_id=0, has_side_effects=True, vmem_limit_bytes=56 << 20),
    )(table, features, w_query, w_key_value.reshape(D, 2 * D), edges, cols_out)


def solution(mesh):
    return jax.shard_map(
        local,
        mesh=mesh,
        in_specs=(
            P(("node", "head"), None),
            P(),
            P(),
            P("head"),
            P("head"),
            P("node", None),
            P("node", None, None),
            P("node", None, None),
        ),
        out_specs=P(("node", "head"), None),
        check_vma=False,
    )
```

```python
import functools
import math

import jax
import jax.numpy as jnp
from jax import lax
from jax.experimental import pallas as pl
from jax.experimental.pallas import tpu as pltpu
from jax.sharding import PartitionSpec as P

HEADS = 8
HDIM = 64
D = 512
TILE = 128
HT = 2
LPR = 8
MATCH = 4
ET = 16
RT = 32
CHUNK = 4
NODES = 64
MESH = pl.DeviceIdType.MESH
F32 = jnp.float32
BF16 = jnp.bfloat16
DISTANCES = (1, 7, 2, 6, 3, 5, 4)
BITS = tuple(m * 6 // 4 for m in range(MATCH))
NONE = ET
EARLY = 1
LATE = 2


def low_lanes(rows):
    return lax.broadcasted_iota(jnp.int32, (rows, TILE), 1) < HDIM


def half_turn(x):
    return pltpu.roll(x, HDIM, 1)


def contract_last(a, b):
    return lax.dot_general(a, b, (((1,), (1,)), ((), ())), preferred_element_type=F32)


def weigh(q, keys):
    return jnp.exp(jnp.clip(contract_last(q, keys), -5.0, 5.0)).astype(BF16)


def with_ones(kv):
    return jnp.where(low_lanes(kv.shape[0]), jnp.ones_like(kv), kv)


def kernel(
    local_cols, exp_rows, exp_cols, feat, w_q, w_kv, e_local, e_expand, cols_out, out,
    send_kv, send_q, kv, halo, vo, q_in, q_local, q_expand, cols_in, cols_smem,
    send_x, kv_x, kv_y, acc, seg, send_o, o_in, edges, last, prev,
    kv_ss, kv_rs, q_ss, q_rs, c_ss, c_rs, c_local, h_ss, h_rs, x_ss, x_rs, y_ss, y_rs, o_ss, o_rs,
):
    node = lax.axis_index("node")
    me = lax.axis_index("head")
    half = CHUNK * TILE // 2
    low_half = low_lanes(half)
    picked = tuple(m for m in range(MATCH) if m != EARLY)

    def around(d):
        return lax.rem(me + d, HEADS)

    def on_z(d):
        return (node, around(d))

    def matched(m):
        return (lax.bitwise_xor(node, jnp.int32(1 << BITS[m])), me)

    def beside(d):
        return (lax.rem(node + d + NODES, NODES), me)

    def remote(src, dst, send_sem, recv_sem, device):
        return pltpu.make_async_remote_copy(
            src_ref=src, dst_ref=dst, send_sem=send_sem, recv_sem=recv_sem, device_id=device, device_id_type=MESH)

    def z_copies(src, dst, send_sems, recv_sems):
        return [remote(src.at[around(d)], dst, send_sems.at[i], recv_sems.at[i], on_z(d)) for i, d in enumerate(DISTANCES)]

    barrier = pltpu.get_barrier_semaphore()
    greeted = [on_z(d) for d in DISTANCES]
    greeted += [matched(m) for m in range(MATCH)]
    greeted += [beside(1), beside(-1)]
    for device in greeted:
        pl.semaphore_signal(barrier, inc=1, device_id=device, device_id_type=MESH)

    features = feat[...]
    low = low_lanes(CHUNK * TILE)
    wide = 2 * TILE
    for quad in range(HEADS // 4):
        at = quad * wide
        keys = jnp.dot(features, w_kv[:, at : at + wide], preferred_element_type=F32)
        values = jnp.dot(features, w_kv[:, D + at : D + at + wide], preferred_element_type=F32)
        for i in range(2):
            k, v = keys[:, i * TILE : (i + 1) * TILE], values[:, i * TILE : (i + 1) * TILE]
            head = 4 * quad + 2 * i
            send_kv[head] = jnp.where(low, k, half_turn(v)).astype(BF16).reshape(CHUNK, TILE, TILE)
            send_kv[head + 1] = jnp.where(low, half_turn(k), v).astype(BF16).reshape(CHUNK, TILE, TILE)

    pl.semaphore_wait(barrier, len(greeted))

    kv_copies = z_copies(send_kv, kv.at[pl.ds(HT + CHUNK * me, CHUNK)], kv_ss, kv_rs)
    for copy in kv_copies:
        copy.start()
    col_copies = {m: remote(cols_out, cols_in.at[m], c_ss.at[m], c_rs.at[m], matched(m)) for m in picked}
    for copy in col_copies.values():
        copy.start()
    forwards = [remote(send_kv.at[me], kv_y.at[pl.ds(CHUNK * me, CHUNK)], y_ss.at[0], y_rs.at[0], matched(EARLY))]
    forwards[0].start()
    kv[pl.ds(HT + CHUNK * me, CHUNK)] = send_kv[me]

    for pair in range(HEADS // 2):
        queries = jnp.dot(features, w_q[:, pair * TILE : (pair + 1) * TILE], preferred_element_type=F32)
        top, bottom = queries[:half], queries[half:]
        send_q[2 * pair] = jnp.where(low_half, top, half_turn(bottom)).astype(BF16)
        send_q[2 * pair + 1] = jnp.where(low_half, half_turn(top), bottom).astype(BF16)
    q_copies = z_copies(send_q, q_in.at[me], q_ss, q_rs)
    q_in[me] = send_q[me]

    edges[...] = jnp.zeros_like(edges)
    edges[0:1, :HDIM] = e_local[...] * (1.0 / math.sqrt(HDIM))
    edges[1:2, :HDIM] = e_expand[...] * (1.0 / math.sqrt(HDIM))
    for m in range(MATCH):
        seg[m, NONE] = jnp.zeros((TILE, TILE), F32)

    def link(m, carry):
        rows = [exp_rows[0, m, e] for e in range(ET)]
        for e in range(ET):
            found = jnp.int32(NONE)
            for j in range(e):
                found = jnp.where(rows[j] == rows[e], j, found)
            prev[m * ET + e] = found
        return carry

    lax.fori_loop(0, MATCH, link, 0)

    def find(t, carry):
        for m in range(MATCH):
            found = jnp.int32(NONE)
            for e in range(ET):
                found = jnp.where(exp_rows[0, m, e] == t, e, found)
            last[m * RT + t] = found
        return carry

    lax.fori_loop(0, RT, find, 0)

    for i, d in enumerate(DISTANCES):
        kv_copies[i].wait_recv()
        source = around(HEADS - d)
        copy = remote(
            kv.at[pl.ds(HT + CHUNK * source, CHUNK)], kv_y.at[pl.ds(CHUNK * source, CHUNK)],
            y_ss.at[i + 1], y_rs.at[i + 1], matched(EARLY))
        copy.start()
        forwards.append(copy)

    for m in picked:
        col_copies[m].wait()
        local = pltpu.make_async_copy(cols_in.at[m], cols_smem.at[m], c_local.at[m])
        local.start()
        local.wait()

    x_copies = {}

    def send_picked(m):
        for e in range(ET):
            send_x[m, e] = kv[HT + cols_smem[m, m, e]]
        x_copies[m] = remote(send_x.at[m], kv_x.at[m], x_ss.at[m], x_rs.at[m], matched(m))
        x_copies[m].start()

    send_picked(LATE)
    halo_copies = [
        remote(kv.at[pl.ds(RT, HT)], halo.at[0], h_ss.at[0], h_rs.at[0], beside(1)),
        remote(kv.at[pl.ds(HT, HT)], halo.at[1], h_ss.at[1], h_rs.at[1], beside(-1)),
    ]
    for copy in halo_copies:
        copy.start()
    for copy in q_copies:
        copy.start()
    for m in picked:
        if m != LATE:
            send_picked(m)

    def own_values(i, carry):
        vo[HT + i] = with_ones(kv[HT + i])
        return carry

    lax.fori_loop(0, RT, own_values, 0)

    for copy in halo_copies:
        copy.wait()
    kv[:HT] = halo[0]
    kv[HT + RT :] = halo[1]
    inside = (jnp.where(node > 0, 1.0, 0.0).astype(F32), jnp.where(node < NODES - 1, 1.0, 0.0).astype(F32))
    for i in range(HT):
        vo[i] = (with_ones(halo[0, i]).astype(F32) * inside[0]).astype(BF16)
        vo[HT + RT + i] = (with_ones(halo[1, i]).astype(F32) * inside[1]).astype(BF16)

    def unpack(z):
        packed = q_in[z].astype(F32)
        turned = half_turn(packed)
        for row, target in ((0, q_local), (1, q_expand)):
            scaling = jnp.broadcast_to(edges[row : row + 1, :], (half, TILE))
            for part, source in ((0, packed), (1, turned)):
                scaled = jnp.where(low_half, source * scaling, 0.0).astype(BF16)
                target[pl.ds(CHUNK * z + 2 * part, 2)] = scaled.reshape(2, TILE, TILE)

    def local_tiles(z):
        unpack(z)
        for i in range(CHUNK):
            t = CHUNK * z + i
            slots = [local_cols[t, s] for s in range(LPR)]
            keys = jnp.concatenate([kv[c] for c in slots], axis=0)
            values = jnp.concatenate([vo[c] for c in slots], axis=0)
            acc[t] = jnp.dot(weigh(q_local[t], keys), values, preferred_element_type=F32)

    local_tiles(me)
    for i, d in enumerate(DISTANCES):
        q_copies[i].wait()
        local_tiles(around(HEADS - d))

    for copy in forwards:
        copy.wait()

    def expander(m):
        for e in range(ET):
            keys = kv_y[exp_cols[0, m, e]] if m == EARLY else kv_x[m, e]
            q = q_expand[exp_rows[0, m, e]]
            seg[m, e] = jnp.dot(weigh(q, keys), with_ones(keys), preferred_element_type=F32) + seg[m, prev[m * ET + e]]

    order = [EARLY] + [m for m in picked if m != LATE]
    for m in order:
        if m != EARLY:
            x_copies[m].wait()
        expander(m)

    def gather_totals(t, carry):
        total = acc[t]
        for m in order:
            total += seg[m, last[m * RT + t]]
        acc[t] = total
        return carry

    lax.fori_loop(0, RT, gather_totals, 0)
    x_copies[LATE].wait()
    expander(LATE)

    def finish(z):
        tiles = []
        for i in range(CHUNK):
            t = CHUNK * z + i
            total = acc[t] + seg[LATE, last[LATE * RT + t]]
            tiles.append(total / half_turn(total))
        top = half_turn(jnp.concatenate(tiles[:2], axis=0))
        bottom = jnp.concatenate(tiles[2:], axis=0)
        send_o[z] = jnp.where(low_half, top, bottom).astype(BF16)

    o_copies = z_copies(send_o, o_in.at[me], o_ss, o_rs)
    for i in reversed(range(len(DISTANCES))):
        finish(around(DISTANCES[i]))
        o_copies[i].start()
    finish(me)
    o_in[me] = send_o[me]
    for copy in o_copies:
        copy.wait()
    for copy in kv_copies:
        copy.wait_send()
    for pair in range(HEADS // 2):
        a, b = o_in[2 * pair].astype(F32), o_in[2 * pair + 1].astype(F32)
        out[:half, pair * TILE : (pair + 1) * TILE] = jnp.where(low_half, a, half_turn(b)).astype(BF16)
        out[half:, pair * TILE : (pair + 1) * TILE] = jnp.where(low_half, half_turn(a), b).astype(BF16)


def local(features, w_query, w_key_value, edge_local, edge_expand, local_cols, exp_rows, exp_cols):
    smem = pl.BlockSpec(memory_space=pltpu.SMEM)
    vmem = pl.BlockSpec(memory_space=pltpu.VMEM)
    n = len(DISTANCES)
    half = CHUNK * TILE // 2
    dma = pltpu.SemaphoreType.DMA
    return pl.pallas_call(
        kernel,
        name="exphormer",
        out_shape=jax.ShapeDtypeStruct((CHUNK * TILE, D), BF16),
        in_specs=[smem] * 3 + [vmem] * 6,
        out_specs=vmem,
        scratch_shapes=[
            pltpu.VMEM((HEADS, CHUNK, TILE, TILE), BF16),
            pltpu.VMEM((HEADS, half, TILE), BF16),
            pltpu.VMEM((RT + 2 * HT, TILE, TILE), BF16),
            pltpu.VMEM((2, HT, TILE, TILE), BF16),
            pltpu.VMEM((RT + 2 * HT, TILE, TILE), BF16),
            pltpu.VMEM((HEADS, half, TILE), BF16),
            pltpu.VMEM((RT, TILE, TILE), BF16),
            pltpu.VMEM((RT, TILE, TILE), BF16),
            pltpu.VMEM((MATCH, MATCH, ET), jnp.int32),
            pltpu.SMEM((MATCH, MATCH, ET), jnp.int32),
            pltpu.VMEM((MATCH, ET, TILE, TILE), BF16),
            pltpu.VMEM((MATCH, ET, TILE, TILE), BF16),
            pltpu.VMEM((RT, TILE, TILE), BF16),
            pltpu.VMEM((RT, TILE, TILE), F32),
            pltpu.VMEM((MATCH, ET + 1, TILE, TILE), F32),
            pltpu.VMEM((HEADS, half, TILE), BF16),
            pltpu.VMEM((HEADS, half, TILE), BF16),
            pltpu.VMEM((2, TILE), F32),
            pltpu.SMEM((MATCH * RT,), jnp.int32),
            pltpu.SMEM((MATCH * ET,), jnp.int32),
            dma((n,)), dma((n,)), dma((n,)), dma((n,)),
            dma((MATCH,)), dma((MATCH,)), dma((MATCH,)),
            dma((2,)), dma((2,)), dma((MATCH,)), dma((MATCH,)), dma((n + 1,)), dma((n + 1,)), dma((n,)), dma((n,)),
        ],
        compiler_params=pltpu.CompilerParams(
            collective_id=0, has_side_effects=True, vmem_limit_bytes=56 << 20),
    )(local_cols, exp_rows, exp_cols, features, w_query, w_key_value.reshape(D, 2 * D),
      edge_local.reshape(1, HDIM), edge_expand.reshape(1, HDIM), exp_cols.reshape(MATCH, ET))


def solution(mesh):
    return jax.shard_map(
        local,
        mesh=mesh,
        in_specs=(
            P(("node", "head"), None),
            P(),
            P(),
            P("head"),
            P("head"),
            P("node", None),
            P("node", None, None),
            P("node", None, None),
        ),
        out_specs=P(("node", "head"), None),
        check_vma=False,
    )
```

```python
import functools
import math

import jax
import jax.numpy as jnp
from jax import lax
from jax.experimental import pallas as pl
from jax.experimental.pallas import tpu as pltpu
from jax.sharding import PartitionSpec as P

HEADS = 8
HDIM = 64
D = 512
TILE = 128
HT = 2
LPR = 8
MATCH = 4
ET = 16
RT = 32
PIECES = 4
CHUNK = 4
NODES = 64
MESH = pl.DeviceIdType.MESH
F32 = jnp.float32
BF16 = jnp.bfloat16
DISTANCES = (1, 7, 2, 6, 3, 5, 4)
BITS = tuple(m * 6 // 4 for m in range(MATCH))
NONE = ET
EARLY = 1
LATE = 2


def low_lanes(rows):
    return lax.broadcasted_iota(jnp.int32, (rows, TILE), 1) < HDIM


def half_turn(x):
    return pltpu.roll(x, HDIM, 1)


def contract_last(a, b):
    return lax.dot_general(a, b, (((1,), (1,)), ((), ())), preferred_element_type=F32)


def weigh(q, keys):
    return jnp.exp(jnp.clip(contract_last(q, keys), -5.0, 5.0)).astype(BF16)


def with_ones(kv):
    return jnp.where(low_lanes(kv.shape[0]), jnp.ones_like(kv), kv)


def kernel(
    local_cols, exp_rows, exp_cols, feat_hbm, w_q_hbm, w_kv_hbm, e_local, e_expand, cols_out, out,
    feat, w_q, w_kv, in_sem,
    send_kv, send_q, kv, halo, vo, q_in, q_local, q_expand, cols_in, cols_smem,
    send_x, kv_x, kv_y, acc, seg, send_o, o_in, edges, last, prev,
    kv_ss, kv_rs, q_ss, q_rs, c_ss, c_rs, c_local, h_ss, h_rs, x_ss, x_rs, y_ss, y_rs, o_ss, o_rs,
):
    node = lax.axis_index("node")
    me = lax.axis_index("head")
    half = CHUNK * TILE // 2
    low_half = low_lanes(half)
    picked = tuple(m for m in range(MATCH) if m != EARLY)

    def around(d):
        return lax.rem(me + d, HEADS)

    def on_z(d):
        return (node, around(d))

    def matched(m):
        return (lax.bitwise_xor(node, jnp.int32(1 << BITS[m])), me)

    def beside(d):
        return (lax.rem(node + d + NODES, NODES), me)

    def remote(src, dst, send_sem, recv_sem, device):
        return pltpu.make_async_remote_copy(
            src_ref=src, dst_ref=dst, send_sem=send_sem, recv_sem=recv_sem, device_id=device, device_id_type=MESH)

    def z_copies(src, dst, send_sems, recv_sems):
        return [remote(src.at[around(d)], dst, send_sems.at[i], recv_sems.at[i], on_z(d)) for i, d in enumerate(DISTANCES)]

    loads = []
    for i in range(PIECES):
        rows = pl.ds(i * D // PIECES, D // PIECES)
        for j, (src, dst) in enumerate(((feat_hbm, feat), (w_kv_hbm, w_kv), (w_q_hbm, w_q))):
            loads.append(pltpu.make_async_copy(src.at[rows], dst.at[rows], in_sem.at[j, i]))
            loads[-1].start()

    barrier = pltpu.get_barrier_semaphore()
    greeted = [on_z(d) for d in DISTANCES]
    greeted += [matched(m) for m in range(MATCH)]
    greeted += [beside(1), beside(-1)]
    for device in greeted:
        pl.semaphore_signal(barrier, inc=1, device_id=device, device_id_type=MESH)

    for copy in loads:
        copy.wait()

    features = feat[...]
    low = low_lanes(CHUNK * TILE)
    wide = 2 * TILE
    for quad in range(HEADS // 4):
        at = quad * wide
        keys = jnp.dot(features, w_kv[:, 0, at : at + wide], preferred_element_type=F32)
        values = jnp.dot(features, w_kv[:, 1, at : at + wide], preferred_element_type=F32)
        for i in range(2):
            k, v = keys[:, i * TILE : (i + 1) * TILE], values[:, i * TILE : (i + 1) * TILE]
            head = 4 * quad + 2 * i
            send_kv[head] = jnp.where(low, k, half_turn(v)).astype(BF16).reshape(CHUNK, TILE, TILE)
            send_kv[head + 1] = jnp.where(low, half_turn(k), v).astype(BF16).reshape(CHUNK, TILE, TILE)

    pl.semaphore_wait(barrier, len(greeted))

    kv_copies = z_copies(send_kv, kv.at[pl.ds(HT + CHUNK * me, CHUNK)], kv_ss, kv_rs)
    for copy in kv_copies:
        copy.start()
    col_copies = {m: remote(cols_out, cols_in.at[m], c_ss.at[m], c_rs.at[m], matched(m)) for m in picked}
    for copy in col_copies.values():
        copy.start()
    halo_copies = [
        remote(kv.at[pl.ds(RT, HT)], halo.at[0], h_ss.at[0], h_rs.at[0], beside(1)),
        remote(kv.at[pl.ds(HT, HT)], halo.at[1], h_ss.at[1], h_rs.at[1], beside(-1)),
    ]

    def send_halo(chunk):
        @pl.when(chunk == HEADS - 1)
        def _():
            halo_copies[0].start()

        @pl.when(chunk == 0)
        def _():
            halo_copies[1].start()

    forwards = [remote(send_kv.at[me], kv_y.at[pl.ds(CHUNK * me, CHUNK)], y_ss.at[0], y_rs.at[0], matched(EARLY))]
    forwards[0].start()
    kv[pl.ds(HT + CHUNK * me, CHUNK)] = send_kv[me]
    send_halo(me)

    for pair in range(HEADS // 2):
        queries = jnp.dot(features, w_q[:, pair * TILE : (pair + 1) * TILE], preferred_element_type=F32)
        top, bottom = queries[:half], queries[half:]
        send_q[2 * pair] = jnp.where(low_half, top, half_turn(bottom)).astype(BF16)
        send_q[2 * pair + 1] = jnp.where(low_half, half_turn(top), bottom).astype(BF16)
    q_copies = z_copies(send_q, q_in.at[me], q_ss, q_rs)
    q_in[me] = send_q[me]

    edges[...] = jnp.zeros_like(edges)
    edges[0:1, :HDIM] = e_local[...] * (1.0 / math.sqrt(HDIM))
    edges[1:2, :HDIM] = e_expand[...] * (1.0 / math.sqrt(HDIM))
    for m in range(MATCH):
        seg[m, NONE] = jnp.zeros((TILE, TILE), F32)

    def link(m, carry):
        rows = [exp_rows[0, m, e] for e in range(ET)]
        for e in range(ET):
            found = jnp.int32(NONE)
            for j in range(e):
                found = jnp.where(rows[j] == rows[e], j, found)
            prev[m * ET + e] = found
        return carry

    lax.fori_loop(0, MATCH, link, 0)

    def find(t, carry):
        for m in range(MATCH):
            found = jnp.int32(NONE)
            for e in range(ET):
                found = jnp.where(exp_rows[0, m, e] == t, e, found)
            last[m * RT + t] = found
        return carry

    lax.fori_loop(0, RT, find, 0)

    for i, d in enumerate(DISTANCES):
        kv_copies[i].wait_recv()
        source = around(HEADS - d)
        send_halo(source)
        copy = remote(
            kv.at[pl.ds(HT + CHUNK * source, CHUNK)], kv_y.at[pl.ds(CHUNK * source, CHUNK)],
            y_ss.at[i + 1], y_rs.at[i + 1], matched(EARLY))
        copy.start()
        forwards.append(copy)

    for m in picked:
        col_copies[m].wait()
        local = pltpu.make_async_copy(cols_in.at[m], cols_smem.at[m], c_local.at[m])
        local.start()
        local.wait()

    x_copies = {}

    def send_picked(m):
        for e in range(ET):
            send_x[m, e] = kv[HT + cols_smem[m, m, e]]
        x_copies[m] = remote(send_x.at[m], kv_x.at[m], x_ss.at[m], x_rs.at[m], matched(m))
        x_copies[m].start()

    send_picked(LATE)
    for copy in q_copies:
        copy.start()
    for m in picked:
        if m != LATE:
            send_picked(m)

    def own_values(i, carry):
        vo[HT + i] = with_ones(kv[HT + i])
        return carry

    lax.fori_loop(0, RT, own_values, 0)

    for copy in halo_copies:
        copy.wait()
    kv[:HT] = halo[0]
    kv[HT + RT :] = halo[1]
    inside = (jnp.where(node > 0, 1.0, 0.0).astype(F32), jnp.where(node < NODES - 1, 1.0, 0.0).astype(F32))
    for i in range(HT):
        vo[i] = (with_ones(halo[0, i]).astype(F32) * inside[0]).astype(BF16)
        vo[HT + RT + i] = (with_ones(halo[1, i]).astype(F32) * inside[1]).astype(BF16)

    def unpack(z):
        packed = q_in[z].astype(F32)
        turned = half_turn(packed)
        for row, target in ((0, q_local), (1, q_expand)):
            scaling = jnp.broadcast_to(edges[row : row + 1, :], (half, TILE))
            for part, source in ((0, packed), (1, turned)):
                scaled = jnp.where(low_half, source * scaling, 0.0).astype(BF16)
                target[pl.ds(CHUNK * z + 2 * part, 2)] = scaled.reshape(2, TILE, TILE)

    def local_tiles(z):
        unpack(z)
        for i in range(CHUNK):
            t = CHUNK * z + i
            slots = [local_cols[s, t] for s in range(LPR)]
            keys = jnp.concatenate([kv[c] for c in slots], axis=0)
            values = jnp.concatenate([vo[c] for c in slots], axis=0)
            acc[t] = jnp.dot(weigh(q_local[t], keys), values, preferred_element_type=F32)

    local_tiles(me)
    for i, d in enumerate(DISTANCES):
        q_copies[i].wait()
        local_tiles(around(HEADS - d))

    for copy in forwards:
        copy.wait()

    def expander(m):
        for e in range(ET):
            keys = kv_y[exp_cols[0, m, e]] if m == EARLY else kv_x[m, e]
            q = q_expand[exp_rows[0, m, e]]
            seg[m, e] = jnp.dot(weigh(q, keys), with_ones(keys), preferred_element_type=F32) + seg[m, prev[m * ET + e]]

    order = [EARLY] + [m for m in picked if m != LATE]
    for m in order:
        if m != EARLY:
            x_copies[m].wait()
        expander(m)

    def gather_totals(t, carry):
        total = acc[t]
        for m in order:
            total += seg[m, last[m * RT + t]]
        acc[t] = total
        return carry

    lax.fori_loop(0, RT, gather_totals, 0)
    x_copies[LATE].wait()
    expander(LATE)

    def finish(z):
        tiles = []
        for i in range(CHUNK):
            t = CHUNK * z + i
            total = acc[t] + seg[LATE, last[LATE * RT + t]]
            tiles.append(total / half_turn(total))
        top = half_turn(jnp.concatenate(tiles[:2], axis=0))
        bottom = jnp.concatenate(tiles[2:], axis=0)
        send_o[z] = jnp.where(low_half, top, bottom).astype(BF16)

    o_copies = z_copies(send_o, o_in.at[me], o_ss, o_rs)
    for i in reversed(range(len(DISTANCES))):
        finish(around(DISTANCES[i]))
        o_copies[i].start()
    finish(me)
    o_in[me] = send_o[me]
    for copy in o_copies:
        copy.wait()
    for copy in kv_copies:
        copy.wait_send()
    for pair in range(HEADS // 2):
        a, b = o_in[2 * pair].astype(F32), o_in[2 * pair + 1].astype(F32)
        out[:half, pair * TILE : (pair + 1) * TILE] = jnp.where(low_half, a, half_turn(b)).astype(BF16)
        out[half:, pair * TILE : (pair + 1) * TILE] = jnp.where(low_half, half_turn(a), b).astype(BF16)


def local(features, w_query, w_key_value, edge_local, edge_expand, local_cols, exp_rows, exp_cols):
    smem = pl.BlockSpec(memory_space=pltpu.SMEM)
    vmem = pl.BlockSpec(memory_space=pltpu.VMEM)
    hbm = pl.BlockSpec(memory_space=pltpu.HBM)
    n = len(DISTANCES)
    half = CHUNK * TILE // 2
    dma = pltpu.SemaphoreType.DMA
    return pl.pallas_call(
        kernel,
        name="exphormer",
        out_shape=jax.ShapeDtypeStruct((CHUNK * TILE, D), BF16),
        in_specs=[smem] * 3 + [hbm] * 3 + [vmem] * 3,
        out_specs=vmem,
        scratch_shapes=[
            pltpu.VMEM((D, D), BF16),
            pltpu.VMEM((D, D), BF16),
            pltpu.VMEM((D, 2, D), BF16),
            dma((3, PIECES)),
            pltpu.VMEM((HEADS, CHUNK, TILE, TILE), BF16),
            pltpu.VMEM((HEADS, half, TILE), BF16),
            pltpu.VMEM((RT + 2 * HT, TILE, TILE), BF16),
            pltpu.VMEM((2, HT, TILE, TILE), BF16),
            pltpu.VMEM((RT + 2 * HT, TILE, TILE), BF16),
            pltpu.VMEM((HEADS, half, TILE), BF16),
            pltpu.VMEM((RT, TILE, TILE), BF16),
            pltpu.VMEM((RT, TILE, TILE), BF16),
            pltpu.VMEM((MATCH, MATCH, ET), jnp.int32),
            pltpu.SMEM((MATCH, MATCH, ET), jnp.int32),
            pltpu.VMEM((MATCH, ET, TILE, TILE), BF16),
            pltpu.VMEM((MATCH, ET, TILE, TILE), BF16),
            pltpu.VMEM((RT, TILE, TILE), BF16),
            pltpu.VMEM((RT, TILE, TILE), F32),
            pltpu.VMEM((MATCH, ET + 1, TILE, TILE), F32),
            pltpu.VMEM((HEADS, half, TILE), BF16),
            pltpu.VMEM((HEADS, half, TILE), BF16),
            pltpu.VMEM((2, TILE), F32),
            pltpu.SMEM((MATCH * RT,), jnp.int32),
            pltpu.SMEM((MATCH * ET,), jnp.int32),
            dma((n,)), dma((n,)), dma((n,)), dma((n,)),
            dma((MATCH,)), dma((MATCH,)), dma((MATCH,)),
            dma((2,)), dma((2,)), dma((MATCH,)), dma((MATCH,)), dma((n + 1,)), dma((n + 1,)), dma((n,)), dma((n,)),
        ],
        compiler_params=pltpu.CompilerParams(
            collective_id=0, has_side_effects=True, vmem_limit_bytes=56 << 20),
    )(local_cols.T, exp_rows, exp_cols, features, w_query, w_key_value,
      edge_local.reshape(1, HDIM), edge_expand.reshape(1, HDIM), exp_cols.reshape(MATCH, ET))


def solution(mesh):
    return jax.shard_map(
        local,
        mesh=mesh,
        in_specs=(
            P(("node", "head"), None),
            P(),
            P(),
            P("head"),
            P("head"),
            P("node", None),
            P("node", None, None),
            P("node", None, None),
        ),
        out_specs=P(("node", "head"), None),
        check_vma=False,
    )
```

```python
import functools
import math

import jax
import jax.numpy as jnp
from jax import lax
from jax.experimental import pallas as pl
from jax.experimental.pallas import tpu as pltpu
from jax.sharding import PartitionSpec as P

HEADS = 8
HDIM = 64
D = 512
TILE = 128
HT = 2
LPR = 8
MATCH = 4
ET = 16
RT = 32
PIECES = 4
CHUNK = 4
NODES = 64
MESH = pl.DeviceIdType.MESH
F32 = jnp.float32
BF16 = jnp.bfloat16
DISTANCES = (1, 7, 2, 6, 3, 5, 4)
BITS = tuple(m * 6 // 4 for m in range(MATCH))
NONE = ET
EARLY = 1
SENDING = (2, 1, 3, 0)
LAG = 0


def low_lanes(rows):
    return lax.broadcasted_iota(jnp.int32, (rows, TILE), 1) < HDIM


def half_turn(x):
    return pltpu.roll(x, HDIM, 1)


def contract_last(a, b):
    return lax.dot_general(a, b, (((1,), (1,)), ((), ())), preferred_element_type=F32)


def weigh(q, keys):
    return jnp.exp(jnp.clip(contract_last(q, keys), -5.0, 5.0)).astype(BF16)


def kernel(
    local_cols, exp_rows, exp_cols, feat_hbm, w_q_hbm, w_kv_hbm, e_local, e_expand, cols_out, out,
    feat, w_q, w_kv, send_k, send_v, send_q, send_o, k_in, v_in, q_in, o_in, k_early,
    keys, values, turned_values, halo_out, halo_in, q_local, q_expand, cols_in, cols_smem,
    send_kx, send_vx, kx, vx, acc, seg, edges, last, prev,
    in_sem, k_ss, k_rs, v_ss, v_rs, q_ss, q_rs, o_ss, o_rs,
    c_ss, c_rs, c_local, h_ss, h_rs, kx_ss, kx_rs, vx_ss, vx_rs, y_ss, y_rs,
):
    node = lax.axis_index("node")
    me = lax.axis_index("head")
    half = CHUNK * TILE // 2
    low = low_lanes(TILE)
    low_half = low_lanes(half)
    picked = tuple(m for m in SENDING if m != EARLY)

    def around(d):
        return lax.rem(me + d, HEADS)

    def on_z(d):
        return (node, around(d))

    def matched(m):
        return (lax.bitwise_xor(node, jnp.int32(1 << BITS[m])), me)

    def beside(d):
        return (lax.rem(node + d + NODES, NODES), me)

    def remote(src, dst, send_sem, recv_sem, device):
        return pltpu.make_async_remote_copy(
            src_ref=src, dst_ref=dst, send_sem=send_sem, recv_sem=recv_sem, device_id=device, device_id_type=MESH)

    def z_copies(src, dst, send_sems, recv_sems):
        return [remote(src.at[around(d)], dst, send_sems.at[i], recv_sems.at[i], on_z(d)) for i, d in enumerate(DISTANCES)]

    loads = []
    for i in range(PIECES):
        rows = pl.ds(i * D // PIECES, D // PIECES)
        for j, (src, dst) in enumerate(((feat_hbm, feat), (w_kv_hbm, w_kv), (w_q_hbm, w_q))):
            loads.append(pltpu.make_async_copy(src.at[rows], dst.at[rows], in_sem.at[j, i]))
            loads[-1].start()

    barrier = pltpu.get_barrier_semaphore()
    greeted = [on_z(d) for d in DISTANCES]
    greeted += [matched(m) for m in range(MATCH)]
    greeted += [beside(1), beside(-1)]
    for device in greeted:
        pl.semaphore_signal(barrier, inc=1, device_id=device, device_id_type=MESH)

    for copy in loads:
        copy.wait()
    features = feat[...]
    wide = 2 * TILE

    def project(weights_at, target):
        for quad in range(HEADS // 4):
            product = jnp.dot(features, weights_at(quad * wide), preferred_element_type=F32)
            for i in range(2):
                two = product[:, i * TILE : (i + 1) * TILE]
                top, bottom = two[:half], two[half:]
                head = 4 * quad + 2 * i
                target[head] = jnp.where(low_half, top, half_turn(bottom)).astype(BF16).reshape(2, TILE, TILE)
                target[head + 1] = jnp.where(low_half, half_turn(top), bottom).astype(BF16).reshape(2, TILE, TILE)

    project(lambda at: w_kv[:, 0, at : at + wide], send_k)
    pl.semaphore_wait(barrier, len(greeted))
    k_copies = z_copies(send_k, k_in.at[me], k_ss, k_rs)
    for copy in k_copies:
        copy.start()
    forwards = [remote(send_k.at[me], k_early.at[me], y_ss.at[0], y_rs.at[0], matched(EARLY))]
    forwards[0].start()
    col_copies = {m: remote(cols_out, cols_in.at[m], c_ss.at[m], c_rs.at[m], matched(m)) for m in SENDING}
    for copy in col_copies.values():
        copy.start()
    k_in[me] = send_k[me]

    project(lambda at: w_kv[:, 1, at : at + wide], send_v)
    v_copies = z_copies(send_v, v_in.at[me], v_ss, v_rs)
    v_in[me] = send_v[me]

    def spread(packed, target, at):
        target[pl.ds(at, 2)] = packed
        turned = half_turn(packed.reshape(half, TILE).astype(F32)).astype(BF16)
        target[pl.ds(at + 2, 2)] = turned.reshape(2, TILE, TILE)

    def take_keys(z):
        spread(k_in[z], keys, HT + CHUNK * z)

    take_keys(me)
    for i, d in enumerate(DISTANCES):
        k_copies[i].wait_recv()
        if i >= LAG:
            v_copies[i - LAG].start()
        source = around(HEADS - d)
        copy = remote(k_in.at[source], k_early.at[source], y_ss.at[i + 1], y_rs.at[i + 1], matched(EARLY))
        copy.start()
        forwards.append(copy)
        take_keys(source)
    for copy in v_copies[len(DISTANCES) - LAG :]:
        copy.start()

    for m in SENDING:
        col_copies[m].wait()
        local = pltpu.make_async_copy(cols_in.at[m], cols_smem.at[m], c_local.at[m])
        local.start()
        local.wait()

    def send_picked(m, source, target, arrive, send_sems, recv_sems):
        for i in range(ET // 2):
            first, second = cols_smem[m, m, 2 * i], cols_smem[m, m, 2 * i + 1]
            target[m, i] = jnp.where(low, source[HT + first], source[HT + (second ^ 2)])
        copy = remote(target.at[m], arrive.at[m], send_sems.at[m], recv_sems.at[m], matched(m))
        copy.start()
        return copy

    kx_copies = {m: send_picked(m, keys, send_kx, kx, kx_ss, kx_rs) for m in picked}

    project(lambda at: w_q[:, at : at + wide], send_q)
    q_copies = z_copies(send_q, q_in.at[me], q_ss, q_rs)
    q_in[me] = send_q[me]

    for row, source in ((0, e_local), (1, e_expand)):
        scaled = source[...] * (1.0 / math.sqrt(HDIM))
        edges[row : row + 1, :HDIM] = scaled
        edges[row : row + 1, HDIM:] = scaled
    for m in range(MATCH):
        seg[m, NONE] = jnp.zeros((TILE, TILE), F32)

    def link(m, carry):
        rows = [exp_rows[0, m, e] for e in range(ET)]
        for e in range(ET):
            found = jnp.int32(NONE)
            for j in range(e):
                found = jnp.where(rows[j] == rows[e], j, found)
            prev[m * ET + e] = found
        return carry

    lax.fori_loop(0, MATCH, link, 0)

    def find(t, carry):
        for m in range(MATCH):
            found = jnp.int32(NONE)
            for e in range(ET):
                found = jnp.where(exp_rows[0, m, e] == t, e, found)
            last[m * RT + t] = found
        return carry

    lax.fori_loop(0, RT, find, 0)

    halo_copies = [
        remote(halo_out.at[0], halo_in.at[0], h_ss.at[0], h_rs.at[0], beside(1)),
        remote(halo_out.at[1], halo_in.at[1], h_ss.at[1], h_rs.at[1], beside(-1)),
    ]

    def take_values(z):
        at = HT + CHUNK * z
        spread(v_in[z], turned_values, at)
        for i in range(CHUNK):
            values[at + i] = jnp.where(low, 1.0, turned_values[at + (i ^ 2)]).astype(BF16)

        def send_halo(which, first):
            for i in range(HT):
                halo_out[which, i] = jnp.where(low, keys[HT + first + i], turned_values[HT + ((first + i) ^ 2)])
            halo_copies[which].start()

        @pl.when(z == HEADS - 1)
        def _():
            send_halo(0, RT - HT)

        @pl.when(z == 0)
        def _():
            send_halo(1, 0)

    take_values(me)
    for i, d in enumerate(DISTANCES):
        v_copies[i].wait_recv()
        if i >= LAG:
            q_copies[i - LAG].start()
        take_values(around(HEADS - d))
    for copy in q_copies[len(DISTANCES) - LAG :]:
        copy.start()

    vx_copies = {m: send_picked(m, turned_values, send_vx, vx, vx_ss, vx_rs) for m in SENDING}

    for copy in halo_copies:
        copy.wait()
    inside = (jnp.where(node > 0, 1.0, 0.0).astype(F32), jnp.where(node < NODES - 1, 1.0, 0.0).astype(F32))
    for which, at in ((0, 0), (1, HT + RT)):
        for i in range(HT):
            keys[at + i] = halo_in[which, i]
            values[at + i] = (jnp.where(low, 1.0, halo_in[which, i].astype(F32)) * inside[which]).astype(BF16)

    def unpack(z):
        packed = q_in[z].reshape(half, TILE).astype(F32)
        turned = half_turn(packed)
        zeros = jnp.zeros((half, TILE), BF16)
        for row in range(2):
            scaling = jnp.broadcast_to(edges[row : row + 1, :], (half, TILE))
            for part, source in ((0, packed), (1, turned)):
                scaled = (source * scaling).astype(BF16)
                lower = jnp.where(low_half, scaled, zeros).reshape(2, TILE, TILE)
                if row == 0:
                    q_local[pl.ds(CHUNK * z + 2 * part, 2)] = lower
                else:
                    upper = jnp.where(low_half, zeros, scaled).reshape(2, TILE, TILE)
                    q_expand[0, pl.ds(CHUNK * z + 2 * part, 2)] = lower
                    q_expand[1, pl.ds(CHUNK * z + 2 * (1 - part), 2)] = upper

    def local_tiles(z):
        unpack(z)
        for i in range(CHUNK):
            t = CHUNK * z + i
            slots = [local_cols[s, t] for s in range(LPR)]
            some_keys = jnp.concatenate([keys[c] for c in slots], axis=0)
            some_values = jnp.concatenate([values[c] for c in slots], axis=0)
            acc[t] = jnp.dot(weigh(q_local[t], some_keys), some_values, preferred_element_type=F32)

    local_tiles(me)
    for i, d in enumerate(DISTANCES):
        q_copies[i].wait_recv()
        local_tiles(around(HEADS - d))

    def expander(m):
        for e in range(ET):
            row, i, upper = exp_rows[0, m, e], e // 2, e % 2
            if m == EARLY:
                col = exp_cols[0, m, e]
                weights = weigh(q_expand[(col // 2) % 2, row], k_early[col // CHUNK, col % 2])
            else:
                weights = weigh(q_expand[upper, row], kx[m, i])
            pair = vx[m, i]
            if upper:
                part = jnp.dot(weights, jnp.where(low, jnp.ones_like(pair), pair), preferred_element_type=F32)
            else:
                part = half_turn(jnp.dot(weights, jnp.where(low, pair, jnp.ones_like(pair)), preferred_element_type=F32))
            seg[m, e] = part + seg[m, prev[m * ET + e]]

    for copy in forwards:
        copy.wait()
    order = tuple(reversed(SENDING))
    for m in order:
        if m == order[-1]:
            def gather_totals(t, carry):
                total = acc[t]
                for m in order[:-1]:
                    total += seg[m, last[m * RT + t]]
                acc[t] = total
                return carry

            lax.fori_loop(0, RT, gather_totals, 0)
        if m != EARLY:
            kx_copies[m].wait()
        vx_copies[m].wait()
        expander(m)

    def finish(z):
        tiles = []
        for i in range(CHUNK):
            t = CHUNK * z + i
            total = acc[t] + seg[order[-1], last[order[-1] * RT + t]]
            tiles.append(total / half_turn(total))
        top = half_turn(jnp.concatenate(tiles[:2], axis=0))
        bottom = jnp.concatenate(tiles[2:], axis=0)
        send_o[z] = jnp.where(low_half, top, bottom).astype(BF16).reshape(2, TILE, TILE)

    o_copies = z_copies(send_o, o_in.at[me], o_ss, o_rs)
    for i in reversed(range(len(DISTANCES))):
        finish(around(DISTANCES[i]))
        o_copies[i].start()
    finish(me)
    o_in[me] = send_o[me]
    for copy in o_copies:
        copy.wait()
    for copy in k_copies + v_copies + q_copies:
        copy.wait_send()
    for pair in range(HEADS // 2):
        a, b = (o_in[2 * pair + i].reshape(half, TILE).astype(F32) for i in range(2))
        out[:half, pair * TILE : (pair + 1) * TILE] = jnp.where(low_half, a, half_turn(b)).astype(BF16)
        out[half:, pair * TILE : (pair + 1) * TILE] = jnp.where(low_half, half_turn(a), b).astype(BF16)


def local(features, w_query, w_key_value, edge_local, edge_expand, local_cols, exp_rows, exp_cols):
    smem = pl.BlockSpec(memory_space=pltpu.SMEM)
    vmem = pl.BlockSpec(memory_space=pltpu.VMEM)
    hbm = pl.BlockSpec(memory_space=pltpu.HBM)
    n = len(DISTANCES)
    dma = pltpu.SemaphoreType.DMA
    packed = pltpu.VMEM((HEADS, 2, TILE, TILE), BF16)
    block = pltpu.VMEM((RT + 2 * HT, TILE, TILE), BF16)
    pairs = pltpu.VMEM((MATCH, ET // 2, TILE, TILE), BF16)
    halo = pltpu.VMEM((2, HT, TILE, TILE), BF16)
    return pl.pallas_call(
        kernel,
        name="exphormer",
        out_shape=jax.ShapeDtypeStruct((CHUNK * TILE, D), BF16),
        in_specs=[smem] * 3 + [hbm] * 3 + [vmem] * 3,
        out_specs=vmem,
        scratch_shapes=[
            pltpu.VMEM((D, D), BF16),
            pltpu.VMEM((D, D), BF16),
            pltpu.VMEM((D, 2, D), BF16),
            packed, packed, packed, packed,
            packed, packed, packed, packed, packed,
            block, block, block,
            halo, halo,
            pltpu.VMEM((RT, TILE, TILE), BF16),
            pltpu.VMEM((2, RT, TILE, TILE), BF16),
            pltpu.VMEM((MATCH, MATCH, ET), jnp.int32),
            pltpu.SMEM((MATCH, MATCH, ET), jnp.int32),
            pairs, pairs, pairs, pairs,
            pltpu.VMEM((RT, TILE, TILE), F32),
            pltpu.VMEM((MATCH, ET + 1, TILE, TILE), F32),
            pltpu.VMEM((2, TILE), F32),
            pltpu.SMEM((MATCH * RT,), jnp.int32),
            pltpu.SMEM((MATCH * ET,), jnp.int32),
            dma((3, PIECES)),
            dma((n,)), dma((n,)), dma((n,)), dma((n,)), dma((n,)), dma((n,)), dma((n,)), dma((n,)),
            dma((MATCH,)), dma((MATCH,)), dma((MATCH,)), dma((2,)), dma((2,)),
            dma((MATCH,)), dma((MATCH,)), dma((MATCH,)), dma((MATCH,)), dma((n + 1,)), dma((n + 1,)),
        ],
        compiler_params=pltpu.CompilerParams(
            collective_id=0, has_side_effects=True, vmem_limit_bytes=56 << 20),
    )(local_cols.T, exp_rows, exp_cols, features, w_query, w_key_value,
      edge_local.reshape(1, HDIM), edge_expand.reshape(1, HDIM), exp_cols.reshape(MATCH, ET))


def solution(mesh):
    return jax.shard_map(
        local,
        mesh=mesh,
        in_specs=(
            P(("node", "head"), None),
            P(),
            P(),
            P("head"),
            P("head"),
            P("node", None),
            P("node", None, None),
            P("node", None, None),
        ),
        out_specs=P(("node", "head"), None),
        check_vma=False,
    )
```

```python
import functools
import math

import jax
import jax.numpy as jnp
from jax import lax
from jax.experimental import pallas as pl
from jax.experimental.pallas import tpu as pltpu
from jax.sharding import PartitionSpec as P

HEADS = 8
HDIM = 64
D = 512
TILE = 128
HT = 2
LPR = 8
MATCH = 4
ET = 16
RT = 32
PIECES = 4
CHUNK = 4
NODES = 64
MESH = pl.DeviceIdType.MESH
F32 = jnp.float32
BF16 = jnp.bfloat16
NONE = ET
EARLY = 1
SENDING = (2, 1, 3, 0)
TAKING = 3


STEPS = HEADS - 1


def distance(i):
    return i // 2 + 1 + (i % 2) * (HEADS - 2 - 2 * (i // 2))


def low_lanes(rows):
    return lax.broadcasted_iota(jnp.int32, (rows, TILE), 1) < HDIM


def half_turn(x):
    return pltpu.roll(x, HDIM, 1)


def contract_last(a, b):
    return lax.dot_general(a, b, (((1,), (1,)), ((), ())), preferred_element_type=F32)


def weigh(q, keys):
    return jnp.exp(jnp.clip(contract_last(q, keys), -5.0, 5.0)).astype(BF16)


def kernel(
    local_cols, exp_rows, exp_cols, feat_hbm, w_q_hbm, w_kv_hbm, e_local, e_expand, cols_out, out,
    feat, w_q, w_kv, send_k, send_v, send_q, send_o, k_in, v_in, q_in, o_in, k_early,
    keys, values, turned_values, halo_out, halo_in, q_local, q_expand, cols_in, cols_smem, keys_early,
    send_kx, send_vx, kx, vx, acc, seg, edges, last, prev,
    in_sem, k_ss, k_rs, v_ss, v_rs, q_ss, q_rs, o_ss, o_rs,
    c_ss, c_rs, c_local, h_ss, h_rs, kx_ss, kx_rs, vx_ss, vx_rs, y_ss, y_rs,
):
    node = lax.axis_index("node")
    me = lax.axis_index("head")
    half = CHUNK * TILE // 2
    low = low_lanes(TILE)
    low_half = low_lanes(half)
    picked = tuple(m for m in SENDING if m != EARLY)

    def around(d):
        return lax.rem(me + d, HEADS)

    def on_z(d):
        return (node, around(d))

    def matched(m):
        return (lax.bitwise_xor(node, jnp.left_shift(jnp.int32(1), m * 3 // 2)), me)

    def beside(d):
        return (lax.rem(node + d + NODES, NODES), me)

    def remote(src, dst, send_sem, recv_sem, device):
        return pltpu.make_async_remote_copy(
            src_ref=src, dst_ref=dst, send_sem=send_sem, recv_sem=recv_sem, device_id=device, device_id_type=MESH)

    def z_copy(i, src, dst, sems):
        d = distance(i)
        return remote(src.at[around(d)], dst.at[me], sems[0].at[i], sems[1].at[i], on_z(d))

    def steps(body):
        def step(i, carry):
            body(i, around(HEADS - distance(i)))
            return carry

        lax.fori_loop(0, STEPS, step, 0)

    k_sems, v_sems, q_sems, o_sems = (k_ss, k_rs), (v_ss, v_rs), (q_ss, q_rs), (o_ss, o_rs)

    loads = []
    for j, (src, dst) in enumerate(((feat_hbm, feat), (w_kv_hbm, w_kv), (w_q_hbm, w_q))):
        for i in range(PIECES):
            rows = pl.ds(i * D // PIECES, D // PIECES)
            loads.append(pltpu.make_async_copy(src.at[rows], dst.at[rows], in_sem.at[j, i]))
            loads[-1].start()

    barrier = pltpu.get_barrier_semaphore()
    greeted = [on_z(d) for d in range(1, HEADS)]
    greeted += [matched(m) for m in range(MATCH)]
    greeted += [beside(1), beside(-1)]
    for device in greeted:
        pl.semaphore_signal(barrier, inc=1, device_id=device, device_id_type=MESH)

    for copy in loads[: 2 * PIECES]:
        copy.wait()
    features = feat[...]
    wide = 2 * TILE

    def project(weights_at, target):
        def quarter(quad, carry):
            product = jnp.dot(features, weights_at(pl.ds(pl.multiple_of(quad * wide, wide), wide)), preferred_element_type=F32)
            for i in range(2):
                two = product[:, i * TILE : (i + 1) * TILE]
                top, bottom = two[:half], two[half:]
                head = 4 * quad + 2 * i
                target[head] = jnp.where(low_half, top, half_turn(bottom)).astype(BF16).reshape(2, TILE, TILE)
                target[head + 1] = jnp.where(low_half, half_turn(top), bottom).astype(BF16).reshape(2, TILE, TILE)
            return carry

        lax.fori_loop(0, HEADS // 4, quarter, 0)

    project(lambda at: w_kv[:, 0, at], send_k)
    pl.semaphore_wait(barrier, len(greeted))
    steps(lambda i, source: z_copy(i, send_k, k_in, k_sems).start())

    def forward(i, src, z):
        return remote(src.at[z], k_early.at[z], y_ss.at[i], y_rs.at[i], matched(EARLY))

    forward(STEPS, send_k, me).start()
    col_copies = {m: remote(cols_out, cols_in.at[m], c_ss.at[m], c_rs.at[m], matched(m)) for m in SENDING}
    for copy in col_copies.values():
        copy.start()
    k_in[me] = send_k[me]

    project(lambda at: w_kv[:, 1, at], send_v)
    v_in[me] = send_v[me]

    def spread(packed, target, at):
        target[pl.ds(at, 2)] = packed
        turned = half_turn(packed.reshape(half, TILE).astype(F32)).astype(BF16)
        target[pl.ds(at + 2, 2)] = turned.reshape(2, TILE, TILE)

    def take_keys(z):
        spread(k_in[z], keys, HT + CHUNK * z)

    take_keys(me)

    def on_keys(i, source):
        z_copy(i, send_k, k_in, k_sems).wait_recv()
        z_copy(i, send_v, v_in, v_sems).start()
        forward(i, k_in, source).start()
        take_keys(source)

    steps(on_keys)

    for m in SENDING:
        col_copies[m].wait()
        local = pltpu.make_async_copy(cols_in.at[m], cols_smem.at[m], c_local.at[m])
        local.start()
        local.wait()

    def kx_copy(m):
        return remote(send_kx.at[m], kx.at[m], kx_ss.at[m], kx_rs.at[m], matched(m))

    def vx_copy(m):
        return remote(send_vx.at[m], vx.at[m], vx_ss.at[m], vx_rs.at[m], matched(m))

    def pick(m, source, target):
        for i in range(ET // 2):
            first, second = cols_smem[m, m, 2 * i], cols_smem[m, m, 2 * i + 1]
            target[m, i] = jnp.where(low, source[HT + first], source[HT + (second ^ 2)])

    for m in picked:
        pick(m, keys, send_kx)
        kx_copy(m).start()

    for copy in loads[2 * PIECES :]:
        copy.wait()
    project(lambda at: w_q[:, at], send_q)
    q_in[me] = send_q[me]

    for row, source in ((0, e_local), (1, e_expand)):
        scaled = source[...] * (1.0 / math.sqrt(HDIM))
        edges[row : row + 1, :HDIM] = scaled
        edges[row : row + 1, HDIM:] = scaled
    for m in range(MATCH):
        seg[m, NONE] = jnp.zeros((TILE, TILE), F32)

    def link(m, carry):
        rows = [exp_rows[0, m, e] for e in range(ET)]
        for e in range(ET):
            found = jnp.int32(NONE)
            for j in range(e):
                found = jnp.where(rows[j] == rows[e], j, found)
            prev[m * ET + e] = found
        return carry

    lax.fori_loop(0, MATCH, link, 0)

    def find(t, carry):
        for m in range(MATCH):
            found = jnp.int32(NONE)
            for e in range(ET):
                found = jnp.where(exp_rows[0, m, e] == t, e, found)
            last[m * RT + t] = found
        return carry

    lax.fori_loop(0, RT, find, 0)

    halo_copies = [
        remote(halo_out.at[0], halo_in.at[0], h_ss.at[0], h_rs.at[0], beside(1)),
        remote(halo_out.at[1], halo_in.at[1], h_ss.at[1], h_rs.at[1], beside(-1)),
    ]

    def take_values(z):
        at = HT + CHUNK * z
        spread(v_in[z], turned_values, at)
        for i in range(CHUNK):
            values[at + i] = jnp.where(low, 1.0, turned_values[at + (i ^ 2)]).astype(BF16)

        def send_halo(which, first):
            for i in range(HT):
                halo_out[which, i] = jnp.where(low, keys[HT + first + i], turned_values[HT + ((first + i) ^ 2)])
            halo_copies[which].start()

        @pl.when(z == HEADS - 1)
        def _():
            send_halo(0, RT - HT)

        @pl.when(z == 0)
        def _():
            send_halo(1, 0)

    take_values(me)

    def on_values(i, source):
        z_copy(i, send_v, v_in, v_sems).wait_recv()
        z_copy(i, send_q, q_in, q_sems).start()
        take_values(source)

    steps(on_values)

    for m in SENDING:
        pick(m, turned_values, send_vx)
        vx_copy(m).start()

    forward(STEPS, send_k, me).wait()
    spread(k_early[me], keys_early, CHUNK * me)

    def on_forwarded(i, source):
        forward(i, k_in, source).wait()
        spread(k_early[source], keys_early, CHUNK * source)

    steps(on_forwarded)
    for i in range(ET // 2):
        one, other = exp_cols[0, EARLY, 2 * i], exp_cols[0, EARLY, 2 * i + 1]
        kx[EARLY, i] = jnp.where(low, keys_early[one], keys_early[other ^ 2])

    def unpack(z):
        packed = q_in[z].reshape(half, TILE).astype(F32)
        turned = half_turn(packed)
        zeros = jnp.zeros((half, TILE), BF16)
        for row in range(2):
            scaling = jnp.broadcast_to(edges[row : row + 1, :], (half, TILE))
            for part, source in ((0, packed), (1, turned)):
                scaled = (source * scaling).astype(BF16)
                lower = jnp.where(low_half, scaled, zeros).reshape(2, TILE, TILE)
                if row == 0:
                    q_local[pl.ds(CHUNK * z + 2 * part, 2)] = lower
                else:
                    upper = jnp.where(low_half, zeros, scaled).reshape(2, TILE, TILE)
                    q_expand[0, pl.ds(CHUNK * z + 2 * part, 2)] = lower
                    q_expand[1, pl.ds(CHUNK * z + 2 * (1 - part), 2)] = upper

    def local_tiles(z):
        for i in range(CHUNK):
            t = CHUNK * z + i
            slots = [local_cols[s, t] for s in range(LPR)]
            some_keys = jnp.concatenate([keys[c] for c in slots], axis=0)
            some_values = jnp.concatenate([values[c] for c in slots], axis=0)
            acc[t] = jnp.dot(weigh(q_local[t], some_keys), some_values, preferred_element_type=F32)

    for copy in halo_copies:
        copy.wait()
    inside = (jnp.where(node > 0, 1.0, 0.0).astype(F32), jnp.where(node < NODES - 1, 1.0, 0.0).astype(F32))
    for which, at in ((0, 0), (1, HT + RT)):
        for i in range(HT):
            keys[at + i] = halo_in[which, i]
            values[at + i] = (jnp.where(low, 1.0, halo_in[which, i].astype(F32)) * inside[which]).astype(BF16)

    def on_queries(k, carry):
        i = jnp.maximum(k - 1, 0)

        @pl.when(k > 0)
        def _():
            z_copy(i, send_q, q_in, q_sems).wait_recv()

        z = jnp.where(k > 0, around(HEADS - distance(i)), me)
        unpack(z)
        local_tiles(z)
        return carry

    lax.fori_loop(0, HEADS, on_queries, 0)

    def expander(k, carry):
        m = TAKING * k % MATCH

        @pl.when(k == MATCH - 1)
        def _():
            lax.fori_loop(0, RT, gather_totals, 0)

        @pl.when(m != EARLY)
        def _():
            kx_copy(m).wait()

        vx_copy(m).wait()
        parts = []
        for e in range(ET):
            upper, pair = e % 2, vx[m, e // 2]
            weights = weigh(q_expand[upper, exp_rows[0, m, e]], kx[m, e // 2])
            if upper:
                part = jnp.dot(weights, jnp.where(low, jnp.ones_like(pair), pair), preferred_element_type=F32)
            else:
                part = half_turn(jnp.dot(weights, jnp.where(low, pair, jnp.ones_like(pair)), preferred_element_type=F32))
            parts.append(part)
        for e in range(ET):
            seg[m, e] = parts[e] + seg[m, prev[m * ET + e]]
        return carry

    def gather_totals(t, carry):
        total = acc[t]
        for m in range(MATCH):
            if m != final:
                total += seg[m, last[m * RT + t]]
        acc[t] = total
        return carry

    final = TAKING * (MATCH - 1) % MATCH
    lax.fori_loop(0, MATCH, expander, 0)

    def finish(z):
        tiles = []
        for i in range(CHUNK):
            t = CHUNK * z + i
            total = acc[t] + seg[final, last[final * RT + t]]
            tiles.append(total / half_turn(total))
        top = half_turn(jnp.concatenate(tiles[:2], axis=0))
        bottom = jnp.concatenate(tiles[2:], axis=0)
        send_o[z] = jnp.where(low_half, top, bottom).astype(BF16).reshape(2, TILE, TILE)

    def send_result(k, carry):
        i = jnp.maximum(STEPS - 1 - k, 0)
        z = jnp.where(k < STEPS, around(distance(i)), me)
        finish(z)

        @pl.when(k < STEPS)
        def _():
            z_copy(i, send_o, o_in, o_sems).start()

        return carry

    lax.fori_loop(0, HEADS, send_result, 0)
    o_in[me] = send_o[me]

    def close(i, source):
        z_copy(i, send_o, o_in, o_sems).wait()
        z_copy(i, send_k, k_in, k_sems).wait_send()
        z_copy(i, send_v, v_in, v_sems).wait_send()
        z_copy(i, send_q, q_in, q_sems).wait_send()

    steps(close)
    for pair in range(HEADS // 2):
        a, b = (o_in[2 * pair + i].reshape(half, TILE).astype(F32) for i in range(2))
        out[:half, pair * TILE : (pair + 1) * TILE] = jnp.where(low_half, a, half_turn(b)).astype(BF16)
        out[half:, pair * TILE : (pair + 1) * TILE] = jnp.where(low_half, half_turn(a), b).astype(BF16)


def local(features, w_query, w_key_value, edge_local, edge_expand, local_cols, exp_rows, exp_cols):
    smem = pl.BlockSpec(memory_space=pltpu.SMEM)
    vmem = pl.BlockSpec(memory_space=pltpu.VMEM)
    hbm = pl.BlockSpec(memory_space=pltpu.HBM)
    n = STEPS
    dma = pltpu.SemaphoreType.DMA
    packed = pltpu.VMEM((HEADS, 2, TILE, TILE), BF16)
    block = pltpu.VMEM((RT + 2 * HT, TILE, TILE), BF16)
    pairs = pltpu.VMEM((MATCH, ET // 2, TILE, TILE), BF16)
    halo = pltpu.VMEM((2, HT, TILE, TILE), BF16)
    return pl.pallas_call(
        kernel,
        name="exphormer",
        out_shape=jax.ShapeDtypeStruct((CHUNK * TILE, D), BF16),
        in_specs=[smem] * 3 + [hbm] * 3 + [vmem] * 3,
        out_specs=vmem,
        scratch_shapes=[
            pltpu.VMEM((D, D), BF16),
            pltpu.VMEM((D, D), BF16),
            pltpu.VMEM((D, 2, D), BF16),
            packed, packed, packed, packed,
            packed, packed, packed, packed, packed,
            block, block, block,
            halo, halo,
            pltpu.VMEM((RT, TILE, TILE), BF16),
            pltpu.VMEM((2, RT, TILE, TILE), BF16),
            pltpu.VMEM((MATCH, MATCH, ET), jnp.int32),
            pltpu.SMEM((MATCH, MATCH, ET), jnp.int32),
            pltpu.VMEM((RT, TILE, TILE), BF16),
            pairs, pairs, pairs, pairs,
            pltpu.VMEM((RT, TILE, TILE), F32),
            pltpu.VMEM((MATCH, ET + 1, TILE, TILE), F32),
            pltpu.VMEM((2, TILE), F32),
            pltpu.SMEM((MATCH * RT,), jnp.int32),
            pltpu.SMEM((MATCH * ET,), jnp.int32),
            dma((3, PIECES)),
            dma((n,)), dma((n,)), dma((n,)), dma((n,)), dma((n,)), dma((n,)), dma((n,)), dma((n,)),
            dma((MATCH,)), dma((MATCH,)), dma((MATCH,)), dma((2,)), dma((2,)),
            dma((MATCH,)), dma((MATCH,)), dma((MATCH,)), dma((MATCH,)), dma((n + 1,)), dma((n + 1,)),
        ],
        compiler_params=pltpu.CompilerParams(
            collective_id=0, has_side_effects=True, vmem_limit_bytes=56 << 20),
    )(local_cols.T, exp_rows, exp_cols, features, w_query, w_key_value,
      edge_local.reshape(1, HDIM), edge_expand.reshape(1, HDIM), exp_cols.reshape(MATCH, ET))


def solution(mesh):
    return jax.shard_map(
        local,
        mesh=mesh,
        in_specs=(
            P(("node", "head"), None),
            P(),
            P(),
            P("head"),
            P("head"),
            P("node", None),
            P("node", None, None),
            P("node", None, None),
        ),
        out_specs=P(("node", "head"), None),
        check_vma=False,
    )
```

```python
import functools
import math

import jax
import jax.numpy as jnp
from jax import lax
from jax.experimental import pallas as pl
from jax.experimental.pallas import tpu as pltpu
from jax.sharding import PartitionSpec as P

HEADS = 8
HDIM = 64
D = 512
TILE = 128
HT = 2
LPR = 8
MATCH = 4
ET = 16
RT = 32
PIECES = 4
CHUNK = 4
NODES = 64
MESH = pl.DeviceIdType.MESH
F32 = jnp.float32
BF16 = jnp.bfloat16
NONE = ET
EARLY = 1
SENDING = (2, 1, 3, 0)
TAKING = 3


STEPS = HEADS - 1
AHEAD = 4


def distance(i):
    return i // 2 + 1 + (i % 2) * (HEADS - 2 - 2 * (i // 2))


def low_lanes(rows):
    return lax.broadcasted_iota(jnp.int32, (rows, TILE), 1) < HDIM


def half_turn(x):
    return pltpu.roll(x, HDIM, 1)


def contract_last(a, b):
    return lax.dot_general(a, b, (((1,), (1,)), ((), ())), preferred_element_type=F32)


def with_ones(kv):
    return jnp.where(low_lanes(kv.shape[0]), jnp.ones_like(kv), kv)


def weigh(q, keys):
    return jnp.exp(jnp.clip(contract_last(q, keys), -5.0, 5.0)).astype(BF16)


def kernel(
    local_cols, exp_rows, exp_cols, feat_hbm, w_q_hbm, w_kv_hbm, e_local, e_expand, cols_out, out,
    feat, w_q, w_kv, send_k, send_v, send_q, send_o, k_in, v_in, q_in, o_in, k_early,
    keys, values, turned_values, halo_out, halo_in, q_local, q_expand, cols_in, cols_smem, keys_early,
    send_kx, send_vx, kx, vx, acc, seg, edges, last, prev, listed,
    in_sem, k_ss, k_rs, v_ss, v_rs, q_ss, q_rs, o_ss, o_rs,
    c_ss, c_rs, c_local, h_ss, h_rs, kx_ss, kx_rs, vx_ss, vx_rs, y_ss, y_rs,
):
    node = lax.axis_index("node")
    me = lax.axis_index("head")
    half = CHUNK * TILE // 2
    low = low_lanes(TILE)
    low_half = low_lanes(half)
    picked = tuple(m for m in SENDING if m != EARLY)

    def around(d):
        return lax.rem(me + d, HEADS)

    def on_z(d):
        return (node, around(d))

    def matched(m):
        return (lax.bitwise_xor(node, jnp.left_shift(jnp.int32(1), m * 3 // 2)), me)

    def beside(d):
        return (lax.rem(node + d + NODES, NODES), me)

    def remote(src, dst, send_sem, recv_sem, device):
        return pltpu.make_async_remote_copy(
            src_ref=src, dst_ref=dst, send_sem=send_sem, recv_sem=recv_sem, device_id=device, device_id_type=MESH)

    def z_copy(i, src, dst, sems):
        d = distance(i)
        return remote(src.at[around(d)], dst.at[me], sems[0].at[i], sems[1].at[i], on_z(d))

    def steps(body):
        def step(i, carry):
            body(i, around(HEADS - distance(i)))
            return carry

        lax.fori_loop(0, STEPS, step, 0)

    k_sems, v_sems, q_sems, o_sems = (k_ss, k_rs), (v_ss, v_rs), (q_ss, q_rs), (o_ss, o_rs)

    loads = []
    for j, (src, dst) in enumerate(((feat_hbm, feat), (w_kv_hbm, w_kv), (w_q_hbm, w_q))):
        for i in range(PIECES):
            rows = pl.ds(i * D // PIECES, D // PIECES)
            loads.append(pltpu.make_async_copy(src.at[rows], dst.at[rows], in_sem.at[j, i]))
            loads[-1].start()

    barrier = pltpu.get_barrier_semaphore()
    greeted = [on_z(d) for d in range(1, HEADS)]
    greeted += [matched(m) for m in range(MATCH)]
    greeted += [beside(1), beside(-1)]
    for device in greeted:
        pl.semaphore_signal(barrier, inc=1, device_id=device, device_id_type=MESH)

    for copy in loads[: 2 * PIECES]:
        copy.wait()
    features = feat[...]
    wide = 2 * TILE

    def project(weights_at, target):
        def quarter(quad, carry):
            product = jnp.dot(features, weights_at(pl.ds(pl.multiple_of(quad * wide, wide), wide)), preferred_element_type=F32)
            for i in range(2):
                two = product[:, i * TILE : (i + 1) * TILE]
                top, bottom = two[:half], two[half:]
                head = 4 * quad + 2 * i
                target[head] = jnp.where(low_half, top, half_turn(bottom)).astype(BF16).reshape(2, TILE, TILE)
                target[head + 1] = jnp.where(low_half, half_turn(top), bottom).astype(BF16).reshape(2, TILE, TILE)
            return carry

        lax.fori_loop(0, HEADS // 4, quarter, 0)

    project(lambda at: w_kv[:, 0, at], send_k)
    pl.semaphore_wait(barrier, len(greeted))
    steps(lambda i, source: z_copy(i, send_k, k_in, k_sems).start())

    def forward(i, src, z):
        return remote(src.at[z], k_early.at[z], y_ss.at[i], y_rs.at[i], matched(EARLY))

    forward(STEPS, send_k, me).start()
    col_copies = {m: remote(cols_out, cols_in.at[m], c_ss.at[m], c_rs.at[m], matched(m)) for m in SENDING}
    for copy in col_copies.values():
        copy.start()
    k_in[me] = send_k[me]

    project(lambda at: w_kv[:, 1, at], send_v)
    v_in[me] = send_v[me]

    def spread(packed, target, at):
        target[pl.ds(at, 2)] = packed
        turned = half_turn(packed.reshape(half, TILE).astype(F32)).astype(BF16)
        target[pl.ds(at + 2, 2)] = turned.reshape(2, TILE, TILE)

    def take_keys(z):
        spread(k_in[z], keys, HT + CHUNK * z)

    take_keys(me)

    def take_cols():
        local = [pltpu.make_async_copy(cols_in.at[m], cols_smem.at[m], c_local.at[m]) for m in SENDING]
        for m, copy in zip(SENDING, local):
            col_copies[m].wait()
            copy.start()
        for copy in local:
            copy.wait()

    def on_keys(i, source):
        z_copy(i, send_k, k_in, k_sems).wait_recv()
        z_copy(i, send_v, v_in, v_sems).start()
        forward(i, k_in, source).start()
        take_keys(source)

        @pl.when(i == STEPS // 2)
        def _():
            take_cols()

    steps(on_keys)

    def kx_copy(m):
        return remote(send_kx.at[m], kx.at[m], kx_ss.at[m], kx_rs.at[m], matched(m))

    def vx_copy(m):
        return remote(send_vx.at[m], vx.at[m], vx_ss.at[m], vx_rs.at[m], matched(m))

    def pick(m, source, target):
        for i in range(ET // 2):
            first, second = cols_smem[m, m, 2 * i], cols_smem[m, m, 2 * i + 1]
            target[m, i] = jnp.where(low, source[HT + first], source[HT + (second ^ 2)])

    for m in picked:
        pick(m, keys, send_kx)
        kx_copy(m).start()

    for copy in loads[2 * PIECES :]:
        copy.wait()
    project(lambda at: w_q[:, at], send_q)
    q_in[me] = send_q[me]
    steps(lambda i, source: z_copy(i, send_q, q_in, q_sems).start())

    for row, source in ((0, e_local), (1, e_expand)):
        scaled = source[...] * (1.0 / math.sqrt(HDIM))
        edges[row : row + 1, :HDIM] = scaled
        edges[row : row + 1, HDIM:] = scaled
    for m in range(MATCH):
        seg[m, NONE] = jnp.zeros((TILE, TILE), F32)
    for at in (0, HT + RT):
        keys[pl.ds(at, HT)] = jnp.zeros((HT, TILE, TILE), BF16)
        values[pl.ds(at, HT)] = jnp.zeros((HT, TILE, TILE), BF16)

    def link(m, carry):
        rows = [exp_rows[0, m, e] for e in range(ET)]
        for e in range(ET):
            found = jnp.int32(NONE)
            for j in range(e):
                found = jnp.where(rows[j] == rows[e], j, found)
            prev[m * ET + e] = found
        return carry

    lax.fori_loop(0, MATCH, link, 0)

    def find(t, carry):
        for m in range(MATCH):
            found = jnp.int32(NONE)
            for e in range(ET):
                found = jnp.where(exp_rows[0, m, e] == t, e, found)
            last[m * RT + t] = found
        for h in range(2 * HT):
            inside = node > 0 if h < HT else node < NODES - 1
            times = jnp.int32(0)
            for slot in range(LPR):
                times += jnp.where(local_cols[slot, t] == (h if h < HT else RT + h), 1, 0)
            listed[h * RT + t] = jnp.where(inside, times, 0)
        return carry

    lax.fori_loop(0, RT, find, 0)

    halo_copies = [
        remote(halo_out.at[0], halo_in.at[0], h_ss.at[0], h_rs.at[0], beside(1)),
        remote(halo_out.at[1], halo_in.at[1], h_ss.at[1], h_rs.at[1], beside(-1)),
    ]

    def take_values(z):
        at = HT + CHUNK * z
        spread(v_in[z], turned_values, at)
        for i in range(CHUNK):
            values[at + i] = jnp.where(low, 1.0, turned_values[at + (i ^ 2)]).astype(BF16)

        def send_halo(which, first):
            for i in range(HT):
                halo_out[which, i] = jnp.where(low, keys[HT + first + i], turned_values[HT + ((first + i) ^ 2)])
            halo_copies[which].start()

        @pl.when(z == HEADS - 1)
        def _():
            send_halo(0, RT - HT)

        @pl.when(z == 0)
        def _():
            send_halo(1, 0)

    take_values(me)

    def on_values(i, source):
        z_copy(i, send_v, v_in, v_sems).wait_recv()
        take_values(source)

    steps(on_values)

    for m in SENDING:
        pick(m, turned_values, send_vx)
        vx_copy(m).start()

    def unpack(z):
        packed = q_in[z].reshape(half, TILE).astype(F32)
        turned = half_turn(packed)
        zeros = jnp.zeros((half, TILE), BF16)
        for row in range(2):
            scaling = jnp.broadcast_to(edges[row : row + 1, :], (half, TILE))
            for part, source in ((0, packed), (1, turned)):
                scaled = (source * scaling).astype(BF16)
                lower = jnp.where(low_half, scaled, zeros).reshape(2, TILE, TILE)
                if row == 0:
                    q_local[pl.ds(CHUNK * z + 2 * part, 2)] = lower
                else:
                    upper = jnp.where(low_half, zeros, scaled).reshape(2, TILE, TILE)
                    q_expand[0, pl.ds(CHUNK * z + 2 * part, 2)] = lower
                    q_expand[1, pl.ds(CHUNK * z + 2 * (1 - part), 2)] = upper

    def local_tiles(z):
        totals = []
        for i in range(CHUNK):
            t = CHUNK * z + i
            slots = [local_cols[s, t] for s in range(LPR)]
            some_keys = jnp.concatenate([keys[c] for c in slots], axis=0)
            some_values = jnp.concatenate([values[c] for c in slots], axis=0)
            totals.append(jnp.dot(weigh(q_local[t], some_keys), some_values, preferred_element_type=F32))
        for i in range(CHUNK):
            acc[CHUNK * z + i] = totals[i]

    def chunk_of(k):
        return jnp.where(k > 0, around(HEADS - distance(jnp.maximum(k - 1, 0))), me)

    def on_queries(k, carry):
        @pl.when(k > 0)
        def _():
            z_copy(jnp.maximum(k - 1, 0), send_q, q_in, q_sems).wait_recv()

        unpack(chunk_of(k))

        @pl.when(k < AHEAD)
        def _():
            local_tiles(chunk_of(k))

        return carry

    lax.fori_loop(0, HEADS, on_queries, 0)

    forward(STEPS, send_k, me).wait()
    spread(k_early[me], keys_early, CHUNK * me)

    def on_forwarded(i, source):
        forward(i, k_in, source).wait()
        spread(k_early[source], keys_early, CHUNK * source)

    steps(on_forwarded)
    for i in range(ET // 2):
        one, other = exp_cols[0, EARLY, 2 * i], exp_cols[0, EARLY, 2 * i + 1]
        kx[EARLY, i] = jnp.where(low, keys_early[one], keys_early[other ^ 2])

    def expander(k, carry):
        m = TAKING * k % MATCH

        @pl.when(m != EARLY)
        def _():
            kx_copy(m).wait()

        vx_copy(m).wait()
        parts = []
        for e in range(ET):
            upper, pair = e % 2, vx[m, e // 2]
            weights = weigh(q_expand[upper, exp_rows[0, m, e]], kx[m, e // 2])
            if upper:
                part = jnp.dot(weights, jnp.where(low, jnp.ones_like(pair), pair), preferred_element_type=F32)
            else:
                part = half_turn(jnp.dot(weights, jnp.where(low, pair, jnp.ones_like(pair)), preferred_element_type=F32))
            parts.append(part)
        for e in range(ET):
            seg[m, e] = parts[e] + seg[m, prev[m * ET + e]]
        return carry

    lax.fori_loop(0, MATCH - 2, expander, 0)

    for copy in halo_copies:
        copy.wait()
    outer = halo_in[...].reshape(2 * HT * TILE, TILE)
    outer_values = with_ones(outer)

    def halo_tiles(k, carry):
        z = chunk_of(k)
        weights = weigh(q_local[pl.ds(CHUNK * z, CHUNK)].reshape(CHUNK * TILE, TILE), outer)
        parts = [
            jnp.dot(weights[:, h * TILE : (h + 1) * TILE], outer_values[h * TILE : (h + 1) * TILE], preferred_element_type=F32)
            for h in range(2 * HT)
        ]
        for i in range(CHUNK):
            t = CHUNK * z + i
            total = acc[t]
            for h in range(2 * HT):
                total += parts[h][i * TILE : (i + 1) * TILE] * listed[h * RT + t].astype(F32)
            acc[t] = total
        return carry

    lax.fori_loop(0, AHEAD, halo_tiles, 0)
    inside = (jnp.where(node > 0, 1.0, 0.0).astype(F32), jnp.where(node < NODES - 1, 1.0, 0.0).astype(F32))
    for which, at in ((0, 0), (1, HT + RT)):
        for i in range(HT):
            keys[at + i] = halo_in[which, i]
            values[at + i] = (with_ones(halo_in[which, i]).astype(F32) * inside[which]).astype(BF16)

    def local_rest(k, carry):
        local_tiles(chunk_of(k))
        return carry

    lax.fori_loop(AHEAD, HEADS, local_rest, 0)

    lax.fori_loop(MATCH - 2, MATCH, expander, 0)

    def finish(z):
        tiles = []
        for i in range(CHUNK):
            t = CHUNK * z + i
            total = acc[t]
            for m in range(MATCH):
                total += seg[m, last[m * RT + t]]
            tiles.append(total / half_turn(total))
        top = half_turn(jnp.concatenate(tiles[:2], axis=0))
        bottom = jnp.concatenate(tiles[2:], axis=0)
        send_o[z] = jnp.where(low_half, top, bottom).astype(BF16).reshape(2, TILE, TILE)

    def send_result(k, carry):
        i = jnp.maximum(STEPS - 1 - k, 0)
        z = jnp.where(k < STEPS, around(distance(i)), me)
        finish(z)

        @pl.when(k < STEPS)
        def _():
            z_copy(i, send_o, o_in, o_sems).start()

        return carry

    lax.fori_loop(0, HEADS, send_result, 0)
    o_in[me] = send_o[me]

    def close(i, source):
        z_copy(i, send_o, o_in, o_sems).wait()
        z_copy(i, send_k, k_in, k_sems).wait_send()
        z_copy(i, send_v, v_in, v_sems).wait_send()
        z_copy(i, send_q, q_in, q_sems).wait_send()

    steps(close)
    for pair in range(HEADS // 2):
        a, b = (o_in[2 * pair + i].reshape(half, TILE).astype(F32) for i in range(2))
        out[:half, pair * TILE : (pair + 1) * TILE] = jnp.where(low_half, a, half_turn(b)).astype(BF16)
        out[half:, pair * TILE : (pair + 1) * TILE] = jnp.where(low_half, half_turn(a), b).astype(BF16)


def local(features, w_query, w_key_value, edge_local, edge_expand, local_cols, exp_rows, exp_cols):
    smem = pl.BlockSpec(memory_space=pltpu.SMEM)
    vmem = pl.BlockSpec(memory_space=pltpu.VMEM)
    hbm = pl.BlockSpec(memory_space=pltpu.HBM)
    n = STEPS
    dma = pltpu.SemaphoreType.DMA
    packed = pltpu.VMEM((HEADS, 2, TILE, TILE), BF16)
    block = pltpu.VMEM((RT + 2 * HT, TILE, TILE), BF16)
    pairs = pltpu.VMEM((MATCH, ET // 2, TILE, TILE), BF16)
    halo = pltpu.VMEM((2, HT, TILE, TILE), BF16)
    return pl.pallas_call(
        kernel,
        name="exphormer",
        out_shape=jax.ShapeDtypeStruct((CHUNK * TILE, D), BF16),
        in_specs=[smem] * 3 + [hbm] * 3 + [vmem] * 3,
        out_specs=vmem,
        scratch_shapes=[
            pltpu.VMEM((D, D), BF16),
            pltpu.VMEM((D, D), BF16),
            pltpu.VMEM((D, 2, D), BF16),
            packed, packed, packed, packed,
            packed, packed, packed, packed, packed,
            block, block, block,
            halo, halo,
            pltpu.VMEM((RT, TILE, TILE), BF16),
            pltpu.VMEM((2, RT, TILE, TILE), BF16),
            pltpu.VMEM((MATCH, MATCH, ET), jnp.int32),
            pltpu.SMEM((MATCH, MATCH, ET), jnp.int32),
            pltpu.VMEM((RT, TILE, TILE), BF16),
            pairs, pairs, pairs, pairs,
            pltpu.VMEM((RT, TILE, TILE), F32),
            pltpu.VMEM((MATCH, ET + 1, TILE, TILE), F32),
            pltpu.VMEM((2, TILE), F32),
            pltpu.SMEM((MATCH * RT,), jnp.int32),
            pltpu.SMEM((MATCH * ET,), jnp.int32),
            pltpu.SMEM((2 * HT * RT,), jnp.int32),
            dma((3, PIECES)),
            dma((n,)), dma((n,)), dma((n,)), dma((n,)), dma((n,)), dma((n,)), dma((n,)), dma((n,)),
            dma((MATCH,)), dma((MATCH,)), dma((MATCH,)), dma((2,)), dma((2,)),
            dma((MATCH,)), dma((MATCH,)), dma((MATCH,)), dma((MATCH,)), dma((n + 1,)), dma((n + 1,)),
        ],
        compiler_params=pltpu.CompilerParams(
            collective_id=0, has_side_effects=True, vmem_limit_bytes=56 << 20),
    )(local_cols.T, exp_rows, exp_cols, features, w_query, w_key_value,
      edge_local.reshape(1, HDIM), edge_expand.reshape(1, HDIM), exp_cols.reshape(MATCH, ET))


def solution(mesh):
    return jax.shard_map(
        local,
        mesh=mesh,
        in_specs=(
            P(("node", "head"), None),
            P(),
            P(),
            P("head"),
            P("head"),
            P("node", None),
            P("node", None, None),
            P("node", None, None),
        ),
        out_specs=P(("node", "head"), None),
        check_vma=False,
    )
```

```python
import functools
import math

import jax
import jax.numpy as jnp
from jax import lax
from jax.experimental import pallas as pl
from jax.experimental.pallas import tpu as pltpu
from jax.sharding import PartitionSpec as P

HEADS = 8
HDIM = 64
D = 512
TILE = 128
HT = 2
LPR = 8
MATCH = 4
ET = 16
RT = 32
PIECES = 4
CHUNK = 4
NODES = 64
MESH = pl.DeviceIdType.MESH
F32 = jnp.float32
BF16 = jnp.bfloat16
NONE = ET
EARLY = 1
SENDING = (2, 1, 3, 0)
TAKING = 3


STEPS = HEADS - 1
AHEAD = 4


def distance(i):
    return i // 2 + 1 + (i % 2) * (HEADS - 2 - 2 * (i // 2))


def low_lanes(rows):
    return lax.broadcasted_iota(jnp.int32, (rows, TILE), 1) < HDIM


def half_turn(x):
    return pltpu.roll(x, HDIM, 1)


def contract_last(a, b):
    return lax.dot_general(a, b, (((1,), (1,)), ((), ())), preferred_element_type=F32)


def with_ones(kv):
    return jnp.where(low_lanes(kv.shape[0]), jnp.ones_like(kv), kv)


def weigh(q, keys):
    return jnp.exp(jnp.clip(contract_last(q, keys), -5.0, 5.0)).astype(BF16)


def kernel(
    local_cols, exp_rows, exp_cols, feat_hbm, w_q_hbm, w_kv_hbm, e_local, e_expand, cols_out, out,
    feat, w_q, w_kv, send_k, send_v, send_q, send_o, k_in, v_in, q_in, o_in, k_early,
    keys, values, turned_values, halo_out, halo_in, q_local, q_expand, cols_in, cols_smem, keys_early,
    send_kx, send_vx, kx, vx, acc, seg, edges, last, prev, listed,
    in_sem, k_ss, k_rs, v_ss, v_rs, q_ss, q_rs, o_ss, o_rs,
    c_ss, c_rs, c_local, h_ss, h_rs, kx_ss, kx_rs, vx_ss, vx_rs, y_ss, y_rs,
):
    node = lax.axis_index("node")
    me = lax.axis_index("head")
    half = CHUNK * TILE // 2
    low = low_lanes(TILE)
    low_half = low_lanes(half)
    picked = tuple(m for m in SENDING if m != EARLY)

    def around(d):
        return lax.rem(me + d, HEADS)

    def on_z(d):
        return (node, around(d))

    def matched(m):
        return (lax.bitwise_xor(node, jnp.left_shift(jnp.int32(1), m * 3 // 2)), me)

    def beside(d):
        return (lax.rem(node + d + NODES, NODES), me)

    def remote(src, dst, send_sem, recv_sem, device):
        return pltpu.make_async_remote_copy(
            src_ref=src, dst_ref=dst, send_sem=send_sem, recv_sem=recv_sem, device_id=device, device_id_type=MESH)

    def z_copy(i, src, dst, sems):
        d = distance(i)
        return remote(src.at[around(d)], dst.at[me], sems[0].at[i], sems[1].at[i], on_z(d))

    def steps(body):
        def step(i, carry):
            body(i, around(HEADS - distance(i)))
            return carry

        lax.fori_loop(0, STEPS, step, 0)

    k_sems, v_sems, q_sems, o_sems = (k_ss, k_rs), (v_ss, v_rs), (q_ss, q_rs), (o_ss, o_rs)

    loads = []
    for j, (src, dst) in enumerate(((feat_hbm, feat), (w_kv_hbm, w_kv), (w_q_hbm, w_q))):
        for i in range(PIECES):
            rows = pl.ds(i * D // PIECES, D // PIECES)
            loads.append(pltpu.make_async_copy(src.at[rows], dst.at[rows], in_sem.at[j, i]))
            loads[-1].start()

    barrier = pltpu.get_barrier_semaphore()
    greeted = [on_z(d) for d in range(1, HEADS)]
    greeted += [matched(m) for m in range(MATCH)]
    greeted += [beside(1), beside(-1)]
    for device in greeted:
        pl.semaphore_signal(barrier, inc=1, device_id=device, device_id_type=MESH)

    for copy in loads[: 2 * PIECES]:
        copy.wait()
    features = feat[...]
    wide = 2 * TILE

    def project(weights_at, target):
        def quarter(quad, carry):
            product = jnp.dot(features, weights_at(pl.ds(pl.multiple_of(quad * wide, wide), wide)), preferred_element_type=F32)
            for i in range(2):
                two = product[:, i * TILE : (i + 1) * TILE]
                top, bottom = two[:half], two[half:]
                head = 4 * quad + 2 * i
                target[head] = jnp.where(low_half, top, half_turn(bottom)).astype(BF16).reshape(2, TILE, TILE)
                target[head + 1] = jnp.where(low_half, half_turn(top), bottom).astype(BF16).reshape(2, TILE, TILE)
            return carry

        lax.fori_loop(0, HEADS // 4, quarter, 0)

    project(lambda at: w_kv[:, 0, at], send_k)
    pl.semaphore_wait(barrier, len(greeted))
    steps(lambda i, source: z_copy(i, send_k, k_in, k_sems).start())

    def forward(i, src, z):
        return remote(src.at[z], k_early.at[z], y_ss.at[i], y_rs.at[i], matched(EARLY))

    forward(STEPS, send_k, me).start()
    col_copies = {m: remote(cols_out, cols_in.at[m], c_ss.at[m], c_rs.at[m], matched(m)) for m in SENDING}
    for copy in col_copies.values():
        copy.start()
    k_in[me] = send_k[me]

    project(lambda at: w_kv[:, 1, at], send_v)
    v_in[me] = send_v[me]

    def spread(packed, target, at):
        target[pl.ds(at, 2)] = packed
        turned = half_turn(packed.reshape(half, TILE).astype(F32)).astype(BF16)
        target[pl.ds(at + 2, 2)] = turned.reshape(2, TILE, TILE)

    def take_keys(z):
        spread(k_in[z], keys, HT + CHUNK * z)

    take_keys(me)

    steps(lambda i, source: z_copy(i, send_v, v_in, v_sems).start())

    def take_cols():
        local = [pltpu.make_async_copy(cols_in.at[m], cols_smem.at[m], c_local.at[m]) for m in SENDING]
        for m, copy in zip(SENDING, local):
            col_copies[m].wait()
            copy.start()
        for copy in local:
            copy.wait()

    def on_keys(i, source):
        z_copy(i, send_k, k_in, k_sems).wait_recv()
        forward(i, k_in, source).start()
        take_keys(source)

        @pl.when(i == STEPS // 2)
        def _():
            take_cols()

    steps(on_keys)

    def kx_copy(m):
        return remote(send_kx.at[m], kx.at[m], kx_ss.at[m], kx_rs.at[m], matched(m))

    def vx_copy(m):
        return remote(send_vx.at[m], vx.at[m], vx_ss.at[m], vx_rs.at[m], matched(m))

    def pick(m, source, target):
        for i in range(ET // 2):
            first, second = cols_smem[m, m, 2 * i], cols_smem[m, m, 2 * i + 1]
            target[m, i] = jnp.where(low, source[HT + first], source[HT + (second ^ 2)])

    for m in picked:
        pick(m, keys, send_kx)
        kx_copy(m).start()

    for copy in loads[2 * PIECES :]:
        copy.wait()
    project(lambda at: w_q[:, at], send_q)
    q_in[me] = send_q[me]
    steps(lambda i, source: z_copy(i, send_q, q_in, q_sems).start())

    for row, source in ((0, e_local), (1, e_expand)):
        scaled = source[...] * (1.0 / math.sqrt(HDIM))
        edges[row : row + 1, :HDIM] = scaled
        edges[row : row + 1, HDIM:] = scaled
    for m in range(MATCH):
        seg[m, NONE] = jnp.zeros((TILE, TILE), F32)
    for at in (0, HT + RT):
        keys[pl.ds(at, HT)] = jnp.zeros((HT, TILE, TILE), BF16)
        values[pl.ds(at, HT)] = jnp.zeros((HT, TILE, TILE), BF16)

    def link(m, carry):
        rows = [exp_rows[0, m, e] for e in range(ET)]
        for e in range(ET):
            found = jnp.int32(NONE)
            for j in range(e):
                found = jnp.where(rows[j] == rows[e], j, found)
            prev[m * ET + e] = found
        return carry

    lax.fori_loop(0, MATCH, link, 0)

    def find(t, carry):
        for m in range(MATCH):
            found = jnp.int32(NONE)
            for e in range(ET):
                found = jnp.where(exp_rows[0, m, e] == t, e, found)
            last[m * RT + t] = found
        for h in range(2 * HT):
            inside = node > 0 if h < HT else node < NODES - 1
            times = jnp.int32(0)
            for slot in range(LPR):
                times += jnp.where(local_cols[slot, t] == (h if h < HT else RT + h), 1, 0)
            listed[h * RT + t] = jnp.where(inside, times, 0)
        return carry

    lax.fori_loop(0, RT, find, 0)

    halo_copies = [
        remote(halo_out.at[0], halo_in.at[0], h_ss.at[0], h_rs.at[0], beside(1)),
        remote(halo_out.at[1], halo_in.at[1], h_ss.at[1], h_rs.at[1], beside(-1)),
    ]

    def take_values(z):
        at = HT + CHUNK * z
        spread(v_in[z], turned_values, at)
        for i in range(CHUNK):
            values[at + i] = jnp.where(low, 1.0, turned_values[at + (i ^ 2)]).astype(BF16)

        def send_halo(which, first):
            for i in range(HT):
                halo_out[which, i] = jnp.where(low, keys[HT + first + i], turned_values[HT + ((first + i) ^ 2)])
            halo_copies[which].start()

        @pl.when(z == HEADS - 1)
        def _():
            send_halo(0, RT - HT)

        @pl.when(z == 0)
        def _():
            send_halo(1, 0)

    take_values(me)

    def on_values(i, source):
        z_copy(i, send_v, v_in, v_sems).wait_recv()
        take_values(source)

    steps(on_values)

    for m in SENDING:
        pick(m, turned_values, send_vx)
        vx_copy(m).start()

    def unpack(z):
        packed = q_in[z].reshape(half, TILE).astype(F32)
        turned = half_turn(packed)
        zeros = jnp.zeros((half, TILE), BF16)
        for row in range(2):
            scaling = jnp.broadcast_to(edges[row : row + 1, :], (half, TILE))
            for part, source in ((0, packed), (1, turned)):
                scaled = (source * scaling).astype(BF16)
                lower = jnp.where(low_half, scaled, zeros).reshape(2, TILE, TILE)
                if row == 0:
                    q_local[pl.ds(CHUNK * z + 2 * part, 2)] = lower
                else:
                    upper = jnp.where(low_half, zeros, scaled).reshape(2, TILE, TILE)
                    q_expand[0, pl.ds(CHUNK * z + 2 * part, 2)] = lower
                    q_expand[1, pl.ds(CHUNK * z + 2 * (1 - part), 2)] = upper

    def local_tiles(z):
        totals = []
        for i in range(CHUNK):
            t = CHUNK * z + i
            slots = [local_cols[s, t] for s in range(LPR)]
            some_keys = jnp.concatenate([keys[c] for c in slots], axis=0)
            some_values = jnp.concatenate([values[c] for c in slots], axis=0)
            totals.append(jnp.dot(weigh(q_local[t], some_keys), some_values, preferred_element_type=F32))
        for i in range(CHUNK):
            acc[CHUNK * z + i] = totals[i]

    def chunk_of(k):
        return jnp.where(k > 0, around(HEADS - distance(jnp.maximum(k - 1, 0))), me)

    def on_queries(k, carry):
        @pl.when(k > 0)
        def _():
            z_copy(jnp.maximum(k - 1, 0), send_q, q_in, q_sems).wait_recv()

        unpack(chunk_of(k))

        @pl.when(k < AHEAD)
        def _():
            local_tiles(chunk_of(k))

        return carry

    lax.fori_loop(0, HEADS, on_queries, 0)

    forward(STEPS, send_k, me).wait()
    spread(k_early[me], keys_early, CHUNK * me)

    def on_forwarded(i, source):
        forward(i, k_in, source).wait()
        spread(k_early[source], keys_early, CHUNK * source)

    steps(on_forwarded)
    for i in range(ET // 2):
        one, other = exp_cols[0, EARLY, 2 * i], exp_cols[0, EARLY, 2 * i + 1]
        kx[EARLY, i] = jnp.where(low, keys_early[one], keys_early[other ^ 2])

    def expander(k, carry):
        m = TAKING * k % MATCH

        @pl.when(m != EARLY)
        def _():
            kx_copy(m).wait()

        vx_copy(m).wait()
        parts = []
        for e in range(ET):
            upper, pair = e % 2, vx[m, e // 2]
            weights = weigh(q_expand[upper, exp_rows[0, m, e]], kx[m, e // 2])
            if upper:
                part = jnp.dot(weights, jnp.where(low, jnp.ones_like(pair), pair), preferred_element_type=F32)
            else:
                part = half_turn(jnp.dot(weights, jnp.where(low, pair, jnp.ones_like(pair)), preferred_element_type=F32))
            parts.append(part)
        for e in range(ET):
            seg[m, e] = parts[e] + seg[m, prev[m * ET + e]]
        return carry

    lax.fori_loop(0, MATCH - 2, expander, 0)

    for copy in halo_copies:
        copy.wait()
    outer = halo_in[...].reshape(2 * HT * TILE, TILE)
    outer_values = with_ones(outer)

    def halo_tiles(k, carry):
        z = chunk_of(k)
        weights = weigh(q_local[pl.ds(CHUNK * z, CHUNK)].reshape(CHUNK * TILE, TILE), outer)
        parts = [
            jnp.dot(weights[:, h * TILE : (h + 1) * TILE], outer_values[h * TILE : (h + 1) * TILE], preferred_element_type=F32)
            for h in range(2 * HT)
        ]
        for i in range(CHUNK):
            t = CHUNK * z + i
            total = acc[t]
            for h in range(2 * HT):
                total += parts[h][i * TILE : (i + 1) * TILE] * listed[h * RT + t].astype(F32)
            acc[t] = total
        return carry

    lax.fori_loop(0, AHEAD, halo_tiles, 0)
    inside = (jnp.where(node > 0, 1.0, 0.0).astype(F32), jnp.where(node < NODES - 1, 1.0, 0.0).astype(F32))
    for which, at in ((0, 0), (1, HT + RT)):
        for i in range(HT):
            keys[at + i] = halo_in[which, i]
            values[at + i] = (with_ones(halo_in[which, i]).astype(F32) * inside[which]).astype(BF16)

    def local_rest(k, carry):
        local_tiles(chunk_of(k))
        return carry

    lax.fori_loop(AHEAD, HEADS, local_rest, 0)

    lax.fori_loop(MATCH - 2, MATCH, expander, 0)

    def finish(z):
        tiles = []
        for i in range(CHUNK):
            t = CHUNK * z + i
            total = acc[t]
            for m in range(MATCH):
                total += seg[m, last[m * RT + t]]
            tiles.append(total / half_turn(total))
        top = half_turn(jnp.concatenate(tiles[:2], axis=0))
        bottom = jnp.concatenate(tiles[2:], axis=0)
        send_o[z] = jnp.where(low_half, top, bottom).astype(BF16).reshape(2, TILE, TILE)

    def send_result(k, carry):
        i = jnp.maximum(STEPS - 1 - k, 0)
        z = jnp.where(k < STEPS, around(distance(i)), me)
        finish(z)

        @pl.when(k < STEPS)
        def _():
            z_copy(i, send_o, o_in, o_sems).start()

        return carry

    lax.fori_loop(0, HEADS, send_result, 0)
    o_in[me] = send_o[me]

    def close(i, source):
        z_copy(i, send_o, o_in, o_sems).wait()
        z_copy(i, send_k, k_in, k_sems).wait_send()
        z_copy(i, send_v, v_in, v_sems).wait_send()
        z_copy(i, send_q, q_in, q_sems).wait_send()

    steps(close)
    for pair in range(HEADS // 2):
        a, b = (o_in[2 * pair + i].reshape(half, TILE).astype(F32) for i in range(2))
        out[:half, pair * TILE : (pair + 1) * TILE] = jnp.where(low_half, a, half_turn(b)).astype(BF16)
        out[half:, pair * TILE : (pair + 1) * TILE] = jnp.where(low_half, half_turn(a), b).astype(BF16)


def local(features, w_query, w_key_value, edge_local, edge_expand, local_cols, exp_rows, exp_cols):
    smem = pl.BlockSpec(memory_space=pltpu.SMEM)
    vmem = pl.BlockSpec(memory_space=pltpu.VMEM)
    hbm = pl.BlockSpec(memory_space=pltpu.HBM)
    n = STEPS
    dma = pltpu.SemaphoreType.DMA
    packed = pltpu.VMEM((HEADS, 2, TILE, TILE), BF16)
    block = pltpu.VMEM((RT + 2 * HT, TILE, TILE), BF16)
    pairs = pltpu.VMEM((MATCH, ET // 2, TILE, TILE), BF16)
    halo = pltpu.VMEM((2, HT, TILE, TILE), BF16)
    return pl.pallas_call(
        kernel,
        name="exphormer",
        out_shape=jax.ShapeDtypeStruct((CHUNK * TILE, D), BF16),
        in_specs=[smem] * 3 + [hbm] * 3 + [vmem] * 3,
        out_specs=vmem,
        scratch_shapes=[
            pltpu.VMEM((D, D), BF16),
            pltpu.VMEM((D, D), BF16),
            pltpu.VMEM((D, 2, D), BF16),
            packed, packed, packed, packed,
            packed, packed, packed, packed, packed,
            block, block, block,
            halo, halo,
            pltpu.VMEM((RT, TILE, TILE), BF16),
            pltpu.VMEM((2, RT, TILE, TILE), BF16),
            pltpu.VMEM((MATCH, MATCH, ET), jnp.int32),
            pltpu.SMEM((MATCH, MATCH, ET), jnp.int32),
            pltpu.VMEM((RT, TILE, TILE), BF16),
            pairs, pairs, pairs, pairs,
            pltpu.VMEM((RT, TILE, TILE), F32),
            pltpu.VMEM((MATCH, ET + 1, TILE, TILE), F32),
            pltpu.VMEM((2, TILE), F32),
            pltpu.SMEM((MATCH * RT,), jnp.int32),
            pltpu.SMEM((MATCH * ET,), jnp.int32),
            pltpu.SMEM((2 * HT * RT,), jnp.int32),
            dma((3, PIECES)),
            dma((n,)), dma((n,)), dma((n,)), dma((n,)), dma((n,)), dma((n,)), dma((n,)), dma((n,)),
            dma((MATCH,)), dma((MATCH,)), dma((MATCH,)), dma((2,)), dma((2,)),
            dma((MATCH,)), dma((MATCH,)), dma((MATCH,)), dma((MATCH,)), dma((n + 1,)), dma((n + 1,)),
        ],
        compiler_params=pltpu.CompilerParams(
            collective_id=0, has_side_effects=True, vmem_limit_bytes=56 << 20),
    )(local_cols.T, exp_rows, exp_cols, features, w_query, w_key_value,
      edge_local.reshape(1, HDIM), edge_expand.reshape(1, HDIM), exp_cols.reshape(MATCH, ET))


def solution(mesh):
    return jax.shard_map(
        local,
        mesh=mesh,
        in_specs=(
            P(("node", "head"), None),
            P(),
            P(),
            P("head"),
            P("head"),
            P("node", None),
            P("node", None, None),
            P("node", None, None),
        ),
        out_specs=P(("node", "head"), None),
        check_vma=False,
    )
```
